32 devices in a mesh: group: 2 (over y), col: 16 (over z, x, core).
Axes of the slice: x: 2, y: 2, z: 4, core: 2. Of those that a mesh axis runs over, the one named last changes fastest.
Arguments:
- estimate: float32 [512, 4096], P('group', 'col'), parts along dimension 0, may hold values from 0.2 to 2.4, as said below
- observed: float32 [512, 4096], P('group', 'col'), parts along dimension 0, may hold values from 0 to 4
- background: float32 [512, 4096], P('group', 'col'), parts along dimension 0, may hold values from 0.5 to 1.5
- sensitivity: float32 [512, 4096], P('group', 'col'), parts along dimension 0, may hold values from 0.5 to 2
- weights: float32 [8, 512, 4096], P(None, 'group', 'col'), parts along dimension 1, may hold values from 0.05 to 0.3
- kernels: float32 [8, 129, 129], replicated, as said below
- valid_mask: int32 [512, 4096], P('group', 'col'), parts along dimension 0, may hold values 0 or 1
- counts: int32 [512, 4096], P('group', 'col'), parts along dimension 0, may hold values from 1 to 8
Outputs:
- updated: float32 [512, 4096], P('group', 'col'), parts along dimension 0
The draws below stay inside these ranges and needn't reach their ends.
There are 2 independent parts, one for each index of `group`. The reference program is written for one: setup_inputs(seed, part) draws one part's arguments, and reference() takes and returns one part's arrays. A program takes and returns all parts, laid end to end along the dimension named above; an argument that names none is the same for every part. Nothing has to cross between parts.
Inputs may be any that keep to these rules, and one draw needn't show every extreme that they name: `kernels`: kernel entries are nonnegative. The estimate is positive.
All inputs are finite; a program needn't handle non-finite values. No bound on the sum of `valid_mask` on one device may be relied on, other than what follows from the above.
Results may differ from the reference program's by a relative error of at most 0.0001.
Values sent between devices are 32-bit elements; how exact they have to be, the bound alone decides.
No kernel may reach another device: no remote copies, remote signals or barrier semaphores. Data moves between devices by JAX's collectives and lax.ppermute only.
A program may use at most 128 MiB of HBM per device.

```python
import math
import jax
import jax.numpy as jnp
from jax import lax

COMPONENTS = 8
HALO = 64
COVER = 8
PSF_SIZE = 129
ROWS = 256
COLS = 4096


def draw_kernels(key, part):
    rough = jax.random.uniform(key, (COMPONENTS, 2 * HALO + 1, 2 * HALO + 1), jnp.float32, 0.5, 1.5)
    offsets = (jnp.arange(2 * HALO + 1) - HALO).astype(jnp.float32)
    across = jnp.abs(offsets[:, None] - offsets[None, :])
    along = jnp.abs(offsets[:, None] + offsets[None, :])
    distance = across + 0.25 * along
    scales = HALO * (0.1 + 0.1 * jnp.arange(COMPONENTS).astype(jnp.float32))
    profile = jnp.exp(-distance[None, :, :] / scales[:, None, None])
    profile = profile / (8.0 * scales * scales + 1.0)[:, None, None]
    return rough * profile


def draw_estimate(key, part):
    level_key = jax.random.fold_in(key, 11)
    noise_key = jax.random.fold_in(key, 23)
    levels = jax.random.uniform(level_key, (1, COLS), jnp.float32, 0.25, 2.0)
    noise = jnp.clip(1.0 + 0.1 * jax.random.normal(noise_key, (ROWS, COLS), jnp.float32), 0.8, 1.2)
    return levels * noise


def with_ends(drawn, rng, smallest, high):
    index_at = [jax.random.randint(jax.random.fold_in(rng, axis), (), 0, length) for axis, length in enumerate(drawn.shape)]
    main_axis = drawn.shape.index(max(drawn.shape))
    beside = index_at[:main_axis] + [(index_at[main_axis] + 1) % drawn.shape[main_axis]] + index_at[main_axis + 1:]
    return drawn.at[tuple(index_at)].set(smallest).at[tuple(beside)].set(high)


def block_levels(key, extent, shards, smallest, high):
    loudness, own = 1.0, jax.random.fold_in(key, 6)
    for dim, blocks in shards:
        heights = jnp.exp(jax.random.uniform(jax.random.fold_in(own, dim), (blocks,), jnp.float32, smallest / len(shards), high / len(shards)))
        loudness = loudness * jnp.repeat(heights, extent[dim] // blocks).reshape([-1 if axis == dim else 1 for axis in range(len(extent))])
    return loudness


def setup_inputs(seed: int = 0, part: int = 0) -> dict:
    key_of = jax.random.split(jax.random.key(seed), 9)
    part_splits = jax.random.split(jax.random.fold_in(key_of[8], part), 9)
    return {
        "estimate": draw_estimate(jax.random.fold_in(jax.random.fold_in(key_of[8], part), 71), part),
        "observed": jnp.clip(4.0 * jax.random.uniform(part_splits[1], (ROWS, COLS), jnp.float32) ** block_levels(part_splits[1], (ROWS, COLS), ((1, 16),), -0.2, 0.2), 0.0, 4.0),
        "background": jnp.clip(0.5 + 1.0 * jax.random.uniform(part_splits[2], (ROWS, COLS), jnp.float32) ** block_levels(part_splits[2], (ROWS, COLS), ((1, 16),), -0.2, 0.2), 0.5, 1.5),
        "sensitivity": jnp.clip(jnp.exp(math.log(2.0) - 1.3862944 * jax.random.uniform(part_splits[3], (ROWS, COLS), jnp.float32) ** block_levels(part_splits[3], (ROWS, COLS), ((1, 16),), -0.2, 0.2)), 0.5, 2.0),
        "weights": jnp.clip(0.05 + 0.25 * jax.random.uniform(part_splits[4], (COMPONENTS, ROWS, COLS), jnp.float32) ** block_levels(part_splits[4], (COMPONENTS, ROWS, COLS), ((2, 16),), -0.2, 0.2), 0.05, 0.3),
        "kernels": draw_kernels(jax.random.fold_in(key_of[8], 71), part),
        "valid_mask": with_ends((jax.random.randint(part_splits[6], (ROWS, COLS), 0, 4) < 3).astype(jnp.int32), jax.random.fold_in(part_splits[6], 1), 0, 1),
        "counts": with_ends(jax.random.randint(part_splits[7], (ROWS, COLS), 1, COVER + 1), jax.random.fold_in(part_splits[7], 1), 1, COVER).astype(jnp.int32),
    }


def kernel_spectrum(kernel, full_shape):
    placed = jnp.zeros(full_shape, jnp.float32).at[:PSF_SIZE, :PSF_SIZE].set(kernel)
    placed = jnp.roll(placed, (-HALO, -HALO), axis=(0, 1))
    return jnp.fft.rfft2(placed)


def reference(estimate, observed, background, sensitivity, weights, kernels, valid_mask, counts):
    full_shape = (ROWS + 2 * HALO, COLS + 2 * HALO)

    def padded(values):
        return jnp.pad(values, HALO)

    def cropped(values):
        return values[HALO:HALO + ROWS, HALO:HALO + COLS]

    initial = 0.0 * jnp.fft.rfft2(padded(estimate))

    def forward_step(running, members):
        weight_k, kernel = members
        term = jnp.fft.rfft2(padded(weight_k * estimate)) * kernel_spectrum(kernel, full_shape)
        return running + term, None

    spectrum, _ = lax.scan(forward_step, initial, (weights, kernels))
    blurred = cropped(jnp.fft.irfft2(spectrum, s=full_shape))
    weight_map = valid_mask.astype(jnp.float32) * counts.astype(jnp.float32) / COVER
    ratio_map = weight_map * observed / (blurred + background)
    ratio_spec = jnp.fft.rfft2(padded(ratio_map))

    def adjoint_step(running, members):
        weight_k, kernel = members
        spread_back = cropped(jnp.fft.irfft2(ratio_spec * jnp.conj(kernel_spectrum(kernel, full_shape)), s=full_shape))
        return running + weight_k * spread_back, None

    correction, _ = lax.scan(adjoint_step, jnp.zeros_like(estimate), (weights, kernels))
    return estimate * correction / sensitivity
```

```python
import functools

import jax
import jax.numpy as jnp
import numpy as np
from jax import lax
from jax.experimental import pallas as pl
from jax.experimental.pallas import tpu as pltpu
from jax.sharding import PartitionSpec as P

COVER = 8
LANES = 128
BF16 = jnp.bfloat16
F32 = jnp.float32


def split_table(table):
    table = table.astype(np.float32)
    high = table.astype(jnp.bfloat16)
    low = (table - high.astype(np.float32)).astype(jnp.bfloat16)
    return np.stack([high, low])


def waves(length, places):
    freqs = np.arange(length // 2) + 0.5
    angles = 2.0 * np.pi * freqs[:, None] * np.asarray(places)[None, :] / length
    return np.cos(angles), np.sin(angles)


def row_table(length, places):
    return np.concatenate(waves(length, places), axis=0)


def col_table(length, places):
    cos, sin = waves(length, places)
    parts = []
    for start in range(0, length // 2, LANES):
        stop = min(start + LANES, length // 2)
        parts += [cos[start:stop], sin[start:stop]]
    return np.concatenate(parts, axis=0).T


def split(values):
    high = values.astype(BF16)
    return high, (values - high.astype(F32)).astype(BF16)


def dot(a, b):
    return jnp.dot(a, b, preferred_element_type=F32)


def product(a, b):
    return dot(a[0], b[0]) + (dot(a[0], b[1]) + dot(a[1], b[0]))


def both(ref):
    return ref[0], ref[1]


def half_sign():
    lane = lax.broadcasted_iota(jnp.int32, (1, LANES), 1)
    return jnp.where(lane < LANES // 2, -1.0, 1.0).astype(F32)


def swap(values):
    return pltpu.roll(values, LANES // 2, 1)


def to_complex(plane, half):
    cos, sin = plane[:half], plane[half:]
    cc, cs, cm = cos[:, :128], cos[:, 128:256], cos[:, 256:]
    sc, ss, sm = sin[:, :128], sin[:, 128:256], sin[:, 256:]
    sm = swap(sm) * half_sign()
    return ((cc - ss, cs + sc, cm + sm), (cc + ss, cs - sc, cm - sm))


def from_complex(plus, minus):
    (a, b, m), (c, d, n) = plus, minus
    top = jnp.concatenate([a + c, b + d, m + n], axis=1)
    mixed = swap(n - m) * half_sign()
    low = jnp.concatenate([b - d, c - a, mixed], axis=1)
    return jnp.concatenate([top, low], axis=0)


def edge_kernel(tile, halo, obs, bg, valid, counts, to_left, to_right):
    lane = lax.broadcasted_iota(jnp.int32, (1, LANES), 1)

    def weighted(cols):
        weight_map = valid[:, cols].astype(F32) * counts[:, cols].astype(F32) * (1.0 / COVER)
        return weight_map * obs[:, cols]

    first, last = slice(0, LANES), slice(tile - LANES, tile)
    to_left[...] = jnp.where(lane < halo, weighted(first), swap(bg[:, first]))
    to_right[...] = jnp.where(lane < halo, swap(weighted(last)), bg[:, last])


def blur_kernel(
    half, est, weights, kernels, row_f, col_f, row_h, col_h, row_i, col_i,
    spectrum, to_left, middle, to_right, total,
):
    k = pl.program_id(0)
    step = split(kernels[0])
    step = split(product(step, both(col_h)))
    (ha, hb, hm), (hc, hd, hn) = to_complex(product(both(row_h), step), half)
    lane = lax.broadcasted_iota(jnp.int32, (1, LANES), 1)
    left = lane < LANES // 2
    sign = half_sign()

    def doubled(m):
        other = swap(m)
        return jnp.where(left, m, other), jnp.where(left, other, m) * sign

    hmr, hmi = doubled(hm)
    hnr, hni = doubled(hn)
    for group, (p, m) in enumerate(((ha, hc), (hb, hd), (hmr, hnr), (hmi, hni))):
        spectrum[0, :half, group * LANES:(group + 1) * LANES] = p
        spectrum[0, half:, group * LANES:(group + 1) * LANES] = m

    step = split(weights[0] * est[...])
    step = split(product(both(row_f), step))
    (fa, fb, fm), (fc, fd, fn) = to_complex(product(step, both(col_f)), half)

    @pl.when(k == 0)
    def _():
        total[...] = jnp.zeros_like(total)

    def add(rows, a, b, m, ha, hb, hr, hi):
        total[rows, 0:128] += a * ha - b * hb
        total[rows, 128:256] += a * hb + b * ha
        total[rows, 256:384] += m * hr + swap(m) * hi

    add(slice(0, half), fa, fb, fm, ha, hb, hmr, hmi)
    add(slice(half, 2 * half), fc, fd, fn, hc, hd, hnr, hni)

    @pl.when(k == pl.num_programs(0) - 1)
    def _():
        def parts(rows):
            return total[rows, 0:128], total[rows, 128:256], total[rows, 256:384]

        step = from_complex(parts(slice(0, half)), parts(slice(half, 2 * half)))
        step = split(product(split(step), both(col_i)))
        blurred = product(both(row_i), step)
        to_left[...] = blurred[:, 0:128]
        middle[...] = blurred[:, 128:256]
        to_right[...] = blurred[:, 256:384]


def correct_kernel(
    half, halo, spectrum, weights, est, obs, bg, sens, valid, counts,
    part_l, part_m, part_r, recv_l, recv_r, edge_l, edge_r,
    row_f, col_f, row_i, col_i, updated, held, total,
):
    k = pl.program_id(0)

    @pl.when(k == 0)
    def _():
        lane = lax.broadcasted_iota(jnp.int32, (1, LANES), 1)
        left = lane < halo

        def widened(own, from_left, from_right):
            first, second = swap(own[:, 0:128]), swap(own[:, 128:256])
            return (
                jnp.where(left, from_left, first),
                jnp.where(left, first, second),
                jnp.where(left, second, from_right),
            )

        weight_map = valid[...].astype(F32) * counts[...].astype(F32) * (1.0 / COVER)
        el, er = edge_l[...], edge_r[...]
        num = widened(weight_map * obs[...], el, swap(er))
        back = widened(bg[...], swap(el), er)
        blurred = (
            part_l[...] + recv_l[...],
            part_m[...],
            part_r[...] + recv_r[...],
        )
        ratio = jnp.concatenate(
            [jnp.where(n > 0.0, n / (b + g), 0.0) for n, b, g in zip(num, blurred, back)], axis=1
        )
        step = split(product(both(row_f), split(ratio)))
        plus, minus = to_complex(product(step, both(col_f)), half)
        for rows, (a, b, m) in ((slice(0, half), plus), (slice(half, 2 * half), minus)):
            held[rows, 0:128] = a
            held[rows, 128:256] = b
            held[rows, 256:384] = m
            held[rows, 384:512] = swap(m)
        total[...] = jnp.zeros_like(total)

    def multiplied(rows):
        a, b, m, w = (held[rows, g * 128:(g + 1) * 128] for g in range(4))
        ha, hb, hr, hi = (spectrum[0, rows, g * 128:(g + 1) * 128] for g in range(4))
        return a * ha + b * hb, b * ha - a * hb, m * hr - w * hi

    step = from_complex(multiplied(slice(0, half)), multiplied(slice(half, 2 * half)))
    step = split(product(split(step), both(col_i)))
    total[...] += weights[0] * product(both(row_i), step)

    @pl.when(k == pl.num_programs(0) - 1)
    def _():
        updated[...] = est[...] * total[...] / sens[...]


def whole_block(array):
    zeros = (0,) * array.ndim
    return pl.BlockSpec(array.shape, lambda k: zeros)


def kth_block(array):
    return pl.BlockSpec((1,) + array.shape[1:], lambda k: (k, 0, 0))


def local(estimate, observed, background, sensitivity, weights, kernels, valid_mask, counts):
    rows, cols = estimate.shape
    components, size = kernels.shape[0], kernels.shape[-1]
    halo = (size - 1) // 2
    row_len, col_len = rows + halo, cols + 2 * halo
    half = row_len // 2
    inner_rows, inner_cols = np.arange(rows), np.arange(cols)
    wide_cols = np.arange(-halo, cols + halo)
    offsets = np.arange(-halo, halo + 1)
    row_f = jnp.asarray(split_table(row_table(row_len, inner_rows)))
    row_i = jnp.asarray(split_table(row_table(row_len, inner_rows).T / row_len))
    row_h = jnp.asarray(split_table(row_table(row_len, offsets)))
    col_h = jnp.asarray(split_table(col_table(col_len, offsets)))
    col_f = jnp.asarray(split_table(col_table(col_len, inner_cols)))
    col_w = jnp.asarray(split_table(col_table(col_len, wide_cols)))
    col_iw = jnp.asarray(split_table(col_table(col_len, wide_cols).T * (2.0 / col_len)))
    col_i = jnp.asarray(split_table(col_table(col_len, inner_cols).T * (2.0 / col_len)))

    side = jax.ShapeDtypeStruct((rows, LANES), F32)
    edge_left, edge_right = pl.pallas_call(
        functools.partial(edge_kernel, cols, halo),
        out_shape=(side, side),
        name="edges",
    )(observed, background, valid_mask, counts)

    count = lax.axis_size("col")
    rightward = [(i, i + 1) for i in range(count - 1)]
    leftward = [(i + 1, i) for i in range(count - 1)]
    edge_l = lax.ppermute(edge_right, "col", rightward)
    edge_r = lax.ppermute(edge_left, "col", leftward)

    macs = 3 * components * row_len * col_len * (rows + cols)
    cost = pl.CostEstimate(flops=2 * macs, bytes_accessed=8 * weights.size, transcendentals=0)
    params = pltpu.CompilerParams(vmem_limit_bytes=56 * 2**20)
    args = (estimate, weights, kernels, row_f, col_f, row_h, col_h, row_i, col_iw)
    spectrum_type = jax.ShapeDtypeStruct((components, row_len, col_len + LANES), F32)
    spectrum, part_l, part_m, part_r = pl.pallas_call(
        functools.partial(blur_kernel, half),
        grid=(components,),
        in_specs=[
            kth_block(a) if i in (1, 2) else whole_block(a) for i, a in enumerate(args)
        ],
        out_specs=[kth_block(spectrum_type)] + [whole_block(side)] * 3,
        out_shape=(spectrum_type, side, side, side),
        scratch_shapes=[pltpu.VMEM((row_len, col_len), F32)],
        compiler_params=params,
        cost_estimate=cost,
        name="blur",
    )(*args)

    recv_l = lax.ppermute(part_r, "col", rightward)
    recv_r = lax.ppermute(part_l, "col", leftward)

    args = (
        spectrum, weights, estimate, observed, background, sensitivity, valid_mask, counts,
        part_l, part_m, part_r, recv_l, recv_r, edge_l, edge_r, row_f, col_w, row_i, col_i,
    )
    return pl.pallas_call(
        functools.partial(correct_kernel, half, halo),
        grid=(components,),
        in_specs=[
            kth_block(a) if i in (0, 1) else whole_block(a) for i, a in enumerate(args)
        ],
        out_specs=whole_block(estimate),
        out_shape=jax.ShapeDtypeStruct(estimate.shape, F32),
        scratch_shapes=[
            pltpu.VMEM((row_len, col_len + LANES), F32),
            pltpu.VMEM((rows, cols), F32),
        ],
        compiler_params=params,
        cost_estimate=cost,
        name="correct",
    )(*args)


def solution(mesh):
    tile = P("group", "col")
    placed = (tile, tile, tile, tile, P(None, "group", "col"), P(), tile, tile)
    return jax.shard_map(local, mesh=mesh, in_specs=placed, out_specs=tile, check_vma=False)
```

```python
import functools

import jax
import jax.numpy as jnp
import numpy as np
from jax import lax
from jax.experimental import pallas as pl
from jax.experimental.pallas import tpu as pltpu
from jax.sharding import PartitionSpec as P

COVER = 8
LANES = 128
VMEM_MIB = 32
BF16 = jnp.bfloat16
F32 = jnp.float32


def halves(table):
    table = table.astype(np.float32)
    high = table.astype(jnp.bfloat16)
    return high, (table - high.astype(np.float32)).astype(jnp.bfloat16)


def waves(length, places):
    angles = 2.0 * np.pi * (np.arange(length // 2) + 0.5)[:, None] * np.asarray(places)[None, :] / length
    return np.concatenate([np.cos(angles), np.sin(angles)], axis=0)


def left_table(table):
    high, low = halves(table)
    return jnp.asarray(np.concatenate([high, low, high], axis=1))


def right_table(table):
    high, low = halves(table)
    return jnp.asarray(np.concatenate([high, high, low], axis=0))


def wide_table(table):
    return jnp.asarray(np.concatenate(halves(table), axis=1))


def split(values):
    high = values.astype(BF16)
    return high, (values - high.astype(F32)).astype(BF16)


def dot(a, b):
    return jnp.dot(a, b, preferred_element_type=F32)


def left_product(table, values):
    high, low = split(values)
    return dot(table[...], jnp.concatenate([high, high, low], axis=0))


def right_product(values, table):
    high, low = split(values)
    return dot(jnp.concatenate([high, low, high], axis=1), table[...])


def to_complex(plane):
    half = plane.shape[0] // 2
    cc, cs = plane[:half, :LANES], plane[:half, LANES:]
    sc, ss = plane[half:, :LANES], plane[half:, LANES:]
    return cc - ss, cs + sc, cc + ss, cs - sc


def from_complex(a, b, c, d):
    top = jnp.concatenate([a + c, b + d], axis=1)
    low = jnp.concatenate([b - d, c - a], axis=1)
    return jnp.concatenate([top, low], axis=0)


def store_spectrum(ref, index, parts):
    half = parts[0].shape[0]
    ref[index, :half, :LANES], ref[index, :half, LANES:] = parts[0], parts[1]
    ref[index, half:, :LANES], ref[index, half:, LANES:] = parts[2], parts[3]


def load_spectrum(ref, index):
    half = ref.shape[1] // 2
    return (
        ref[index, :half, :LANES], ref[index, :half, LANES:],
        ref[index, half:, :LANES], ref[index, half:, LANES:],
    )


def swap(values):
    return pltpu.roll(values, LANES // 2, 1)


def side_of(outer):
    core = lax.axis_index("col") % 2
    return core if outer else 1 - core


def side_columns(ref, side):
    return ref[:, pl.ds(pl.multiple_of(side * LANES, LANES), LANES)]


def numerator(obs, valid, counts):
    return valid.astype(F32) * counts.astype(F32) * (1.0 / COVER) * obs


def blur_pair(est_half, weight_of, spectrum_of, row_f, col_f):
    pair = jnp.concatenate([weight_of(i) * est_half for i in range(2)], axis=1)
    rows = left_product(row_f, pair)
    sums = None
    for i in range(2):
        fa, fb, fc, fd = to_complex(right_product(rows[:, i * LANES:(i + 1) * LANES], col_f))
        ha, hb, hc, hd = spectrum_of(i)
        terms = (fa * ha - fb * hb, fa * hb + fb * ha, fc * hc - fd * hd, fc * hd + fd * hc)
        sums = terms if sums is None else tuple(s + t for s, t in zip(sums, terms))
    return sums


def accumulate(ref, first, sums):
    if not first:
        sums = tuple(s + t for s, t in zip(load_spectrum(ref, 0), sums))
    store_spectrum(ref, 0, sums)


def blur_end(side, obs, bg, valid, counts, row_i, col_i, total, edge, packed, middle, window):
    plane = right_product(from_complex(*load_spectrum(total, 0)), col_i)
    window[...] = left_product(row_i, plane)
    edge[...] = side_columns(window, side)
    middle[...] = side_columns(window, 1 - side)
    num = numerator(obs, valid, counts)
    lane = lax.broadcasted_iota(jnp.int32, (1, LANES), 1)
    num = jnp.where(side == 0, num, swap(num))
    back = jnp.where(side == 0, swap(bg), bg)
    packed[...] = jnp.where(lane < LANES // 2, num, back)


def outer_blur(components, *refs):
    inputs, refs = refs[:13], refs[13:]
    (spectrum, edge, middle), refs = refs[:3], refs[3:]
    held, (cos_columns, sin_columns, total, window, done) = refs[:13], refs[13:]
    columns = (cos_columns, sin_columns)
    side = side_of(True)
    half = pl.ds(pl.multiple_of(side * LANES, LANES), LANES)
    copies = []
    for i, (ref, kept) in enumerate(zip(inputs, held)):
        if i >= 7:
            ref = ref.at[:, :, half] if len(ref.shape) == 3 else ref.at[:, half]
        copies.append(pltpu.make_async_copy(ref, kept, done.at[i]))
    for copy in copies:
        copy.start()
    kernels, col_h, row_h, row_f, col_f, col_i, row_i, est, weights, obs, bg, valid, counts = held
    size = kernels.shape[0]
    padded = row_h.shape[1] // 3
    copies[0].wait()
    copies[1].wait()
    flat = kernels[...].reshape(size * components, size)
    plane = right_product(flat, col_h)
    for part, ref in enumerate(columns):
        ref[:size * components] = plane[:, part * LANES:(part + 1) * LANES]
        ref[size * components:] = jnp.zeros(((padded - size) * components, LANES), F32)
    for i in (2, 3, 4, 7, 8):
        copies[i].wait()

    def spectrum_of(k):
        places = pl.ds(k, padded, stride=components)
        rows = jnp.concatenate([ref[places, :] for ref in columns], axis=1)
        parts = to_complex(left_product(row_h, rows))
        store_spectrum(spectrum, k, parts)
        return parts

    for k in range(0, components, 2):
        sums = blur_pair(
            est[...], lambda i: weights[k + i], lambda i: spectrum_of(k + i), row_f, col_f
        )
        accumulate(total, k == 0, sums)
    for i in (5, 6, 9, 10, 11, 12):
        copies[i].wait()
    blur_end(
        side, obs[...], bg[...], valid[...], counts[...], row_i, col_i, total,
        edge.at[:, :LANES], edge.at[:, LANES:], middle, window,
    )


def inner_blur(
    est, obs, bg, valid, counts, weights, spectrum, row_f, col_f, row_i, col_i,
    edge, packed, middle, total, window,
):
    side = side_of(False)
    for k in range(0, weights.shape[0], 2):
        sums = blur_pair(
            side_columns(est, side), lambda i: side_columns(weights.at[k + i], side),
            lambda i: load_spectrum(spectrum, k + i), row_f, col_f,
        )
        accumulate(total, k == 0, sums)
    tiles = (side_columns(ref, side) for ref in (obs, bg, valid, counts))
    blur_end(side, *tiles, row_i, col_i, total, edge, packed, middle, window)


def correct_half(
    outer, est, obs, bg, sens, valid, counts, weights, spectrum, edge, received, packed, middle, other,
    row_f, col_w, row_i, col_i, updated, ratio, held, total, done=None,
):
    side = side_of(outer)
    lane = lax.broadcasted_iota(jnp.int32, (1, LANES), 1)
    left = lane < LANES // 2
    num = numerator(obs[...], valid[...], counts[...])

    def centre(own):
        return jnp.where(left, swap(own[:, :LANES]), swap(own[:, LANES:]))

    def at_edge(own):
        return swap(jnp.where(side == 0, own[:, :LANES], own[:, LANES:]))

    def divided(num, blurred, back):
        return jnp.where(num > 0.0, num / (blurred + back), 0.0)

    packed = packed[...]
    turned = swap(packed)
    from_other = (lane >= LANES // 2) == (side == 1)
    edge_num = jnp.where(from_other, jnp.where(side == 0, packed, turned), at_edge(num))
    edge_back = jnp.where(from_other, jnp.where(side == 0, turned, packed), at_edge(bg[...]))
    first = pl.ds(pl.multiple_of(side * LANES, LANES), LANES)
    second = pl.ds(pl.multiple_of((1 - side) * LANES, LANES), LANES)
    ratio[:, first] = divided(edge_num, edge[...] + received[...], edge_back)
    ratio[:, second] = divided(centre(num), middle[...] + other[...], centre(bg[...]))
    store_spectrum(held, 0, to_complex(right_product(left_product(row_f, ratio[...]), col_w)))

    for k in range(0, weights.shape[0], 2):
        planes = []
        a, b, c, d = load_spectrum(held, 0)
        for i in range(2):
            ha, hb, hc, hd = load_spectrum(spectrum, k + i)
            plane = from_complex(a * ha + b * hb, b * ha - a * hb, c * hc + d * hd, d * hc - c * hd)
            high, low = split(plane)
            both = dot(high, col_i[...])
            planes.append(both[:, :LANES] + (both[:, LANES:] + dot(low, col_i[:, :LANES])))
        pair = left_product(row_i, jnp.concatenate(planes, axis=1))
        sums = (
            side_columns(weights.at[k], side) * pair[:, :LANES]
            + side_columns(weights.at[k + 1], side) * pair[:, LANES:]
        )
        total[...] = sums if k == 0 else total[...] + sums

    result = side_columns(est, side) * total[...] / side_columns(sens, side)
    if done is None:
        updated[...] = result
    else:
        updated[:, first] = result
        updated[:, second] = done[...]


def inner_correct(*refs):
    correct_half(False, *refs)


def outer_correct(*refs):
    edge, received, middle, other, done = refs[8:13]
    correct_half(
        True, *refs[:8], edge.at[:, :LANES], received.at[:, :LANES], received.at[:, LANES:],
        middle, other, *refs[13:], done=done,
    )


def call(kernel, name, flops, args, outs, scratch, space=pltpu.VMEM):
    size = sum(a.size * a.dtype.itemsize for a in args)
    if space is pltpu.HBM:
        args = [pltpu.with_memory_space_constraint(a, pltpu.HBM) for a in args]
    return pl.pallas_call(
        kernel,
        in_specs=[pl.BlockSpec(memory_space=space)] * len(args),
        out_specs=[pl.BlockSpec(memory_space=pltpu.VMEM)] * len(outs),
        out_shape=outs,
        scratch_shapes=scratch,
        compiler_params=pltpu.CompilerParams(vmem_limit_bytes=VMEM_MIB * 2**20),
        cost_estimate=pl.CostEstimate(flops=flops // 100, bytes_accessed=size // 100, transcendentals=0),
        name=name,
    )(*args)


def local(estimate, observed, background, sensitivity, weights, kernels, valid_mask, counts):
    rows, cols = estimate.shape
    components, size = kernels.shape[0], kernels.shape[-1]
    halo = (size - 1) // 2
    half_cols = cols // 2
    row_len, col_len = rows + halo, half_cols + 2 * halo
    inner_rows, inner_cols = np.arange(rows), np.arange(half_cols)
    wide_cols = np.arange(-halo, half_cols + halo)
    offsets = np.arange(-halo, halo + 1)
    padded = -(-size // 16) * 16
    row_h = np.pad(waves(row_len, offsets), ((0, 0), (0, padded - size)))
    row_f = left_table(waves(row_len, inner_rows))
    row_i = left_table(waves(row_len, inner_rows).T / row_len)
    row_h = left_table(row_h)
    col_h = right_table(waves(col_len, offsets).T)
    col_f = right_table(waves(col_len, inner_cols).T)
    col_w = right_table(waves(col_len, wide_cols).T)
    col_iw = right_table(waves(col_len, wide_cols) * (2.0 / col_len))
    col_i = wide_table(waves(col_len, inner_cols) * (2.0 / col_len))

    count = lax.axis_size("col")
    between = [(i, i + 1) for i in range(1, count - 1, 2)]
    between += [(j, i) for i, j in between]
    within = [(i, i ^ 1) for i in range(count)]

    macs = 3 * components * row_len * half_cols * (rows + 2 * col_len)
    plane = jax.ShapeDtypeStruct((rows, LANES), F32)
    wide = jax.ShapeDtypeStruct((rows, 2 * LANES), F32)
    spectra = jax.ShapeDtypeStruct((components, row_len, col_len), F32)
    total = pltpu.VMEM((1, row_len, col_len), F32)
    window = pltpu.VMEM((rows, col_len), F32)
    tiles = (observed, background, valid_mask, counts)
    tables = (col_h, row_h, row_f, col_f, col_iw, row_i)
    turned = jnp.transpose(kernels, (1, 0, 2))
    held = [pltpu.VMEM(a.shape, a.dtype) for a in (turned, *tables)]
    held += [
        pltpu.VMEM(a.shape[:-1] + (half_cols,), a.dtype) for a in (estimate, weights, *tiles)
    ]
    columns = pltpu.VMEM((padded * components, LANES), F32)
    spectrum, edge_o, middle_o = call(
        functools.partial(outer_blur, components), "outer_blur", 4 * macs,
        (turned, *tables, estimate, weights, *tiles), (spectra, wide, plane),
        [*held, columns, columns, total, window, pltpu.SemaphoreType.DMA((len(held),))],
        pltpu.HBM,
    )
    received_o = lax.ppermute(edge_o, "col", between)
    edge_i, packed_i, middle_i = call(
        inner_blur, "inner_blur", 2 * macs,
        (estimate, *tiles, weights, spectrum, row_f, col_f, row_i, col_iw),
        (plane, plane, plane), [total, window],
    )
    received_i = (lax.ppermute(edge_i, "col", within), lax.ppermute(packed_i, "col", within))
    shared = (
        estimate, observed, background, sensitivity, valid_mask, counts, weights, spectrum
    )
    tables = (row_f, col_w, row_i, col_i)
    scratch = [window, total, pltpu.VMEM((rows, LANES), F32)]
    (half,) = call(
        inner_correct, "inner_correct", 2 * macs,
        (*shared, edge_i, *received_i, middle_i, middle_o, *tables), (plane,), scratch,
    )
    (updated,) = call(
        outer_correct, "outer_correct", 2 * macs,
        (*shared, edge_o, received_o, middle_o, middle_i, half, *tables), (wide,), scratch,
    )
    return updated


def solution(mesh):
    tile = P("group", "col")
    placed = (tile, tile, tile, tile, P(None, "group", "col"), P(), tile, tile)
    return jax.shard_map(local, mesh=mesh, in_specs=placed, out_specs=tile, check_vma=False)
```

```python
import functools

import jax
import jax.numpy as jnp
import numpy as np
from jax import lax
from jax.experimental import pallas as pl
from jax.experimental.pallas import tpu as pltpu
from jax.sharding import PartitionSpec as P

COVER = 8
LANES = 128
VMEM_MIB = 32
BF16 = jnp.bfloat16
F32 = jnp.float32


def halves(table):
    table = table.astype(np.float32)
    high = table.astype(jnp.bfloat16)
    return high, (table - high.astype(np.float32)).astype(jnp.bfloat16)


def waves(length, places):
    angles = 2.0 * np.pi * (np.arange(length // 2) + 0.5)[:, None] * np.asarray(places)[None, :] / length
    return np.concatenate([np.cos(angles), np.sin(angles)], axis=0)


def whole_waves(length, places):
    freqs = np.arange(length // 2)
    freqs = np.concatenate([freqs[0::2], freqs[1::2]])
    angles = 2.0 * np.pi * freqs[:, None] * np.asarray(places)[None, :] / length
    sin = np.sin(angles)
    sin[0] = np.cos(np.pi * np.asarray(places))
    return np.cos(angles), sin


def parity_waves(length, places):
    cos, sin = whole_waves(length, places)
    quarter = length // 4
    return (
        np.concatenate([cos[:quarter], sin[:quarter]]),
        np.concatenate([cos[quarter:], sin[quarter:]]),
    )


def left_table(table):
    high, low = halves(table)
    return jnp.asarray(np.concatenate([high, low, high], axis=1))


def right_table(table):
    high, low = halves(table)
    return jnp.asarray(np.concatenate([high, high, low], axis=0))


def wide_table(table):
    return jnp.asarray(np.concatenate(halves(table), axis=1))


def split(values):
    high = values.astype(BF16)
    return high, (values - high.astype(F32)).astype(BF16)


def dot(a, b):
    return jnp.dot(a, b, preferred_element_type=F32)


def left_product(table, values):
    high, low = split(values)
    return dot(table[...], jnp.concatenate([high, high, low], axis=0))


def right_product(values, table):
    high, low = split(values)
    return dot(jnp.concatenate([high, low, high], axis=1), table[...])


def rows_forward(even, odd, values):
    half = even.shape[1] // 3
    quarter = even.shape[0] // 2
    rest = values.shape[0] - half
    first, second, alone = values[:rest], values[half:], values[rest:half]
    e = left_product(even, jnp.concatenate([first + second, alone], axis=0))
    o = left_product(odd, jnp.concatenate([first - second, alone], axis=0))
    return jnp.concatenate([e[:quarter], o[:quarter], e[quarter:], o[quarter:]], axis=0)


def rows_inverse(even, odd, plane, rows):
    quarter = plane.shape[0] // 4
    parts = [plane[i * quarter:(i + 1) * quarter] for i in range(4)]
    e = left_product(even, jnp.concatenate([parts[0], parts[2]], axis=0))
    o = left_product(odd, jnp.concatenate([parts[1], parts[3]], axis=0))
    return jnp.concatenate([e + o, (e - o)[:rows - e.shape[0]]], axis=0)


def fix_first(first, values):
    row = lax.broadcasted_iota(jnp.int32, (8, 1), 0)
    return jnp.concatenate([jnp.where(row == 0, first, values[:8]), values[8:]], axis=0)


def to_complex(plane):
    half = plane.shape[0] // 2
    cc, cs = plane[:half, :LANES], plane[:half, LANES:]
    sc, ss = plane[half:, :LANES], plane[half:, LANES:]
    return (
        fix_first(cc[:8], cc - ss), fix_first(cs[:8], cs + sc),
        fix_first(sc[:8], cc + ss), fix_first(ss[:8], cs - sc),
    )


def from_complex(a, b, c, d):
    top = jnp.concatenate([fix_first(a[:8], a + c), fix_first(b[:8], b + d)], axis=1)
    low = jnp.concatenate([fix_first(c[:8], b - d), fix_first(d[:8], c - a)], axis=1)
    return jnp.concatenate([top, low], axis=0)


def store_spectrum(ref, index, parts):
    half = parts[0].shape[0]
    ref[index, :half, :LANES], ref[index, :half, LANES:] = parts[0], parts[1]
    ref[index, half:, :LANES], ref[index, half:, LANES:] = parts[2], parts[3]


def load_spectrum(ref, index):
    half = ref.shape[1] // 2
    return (
        ref[index, :half, :LANES], ref[index, :half, LANES:],
        ref[index, half:, :LANES], ref[index, half:, LANES:],
    )


def swap(values):
    return pltpu.roll(values, LANES // 2, 1)


def side_of(outer):
    core = lax.axis_index("col") % 2
    return core if outer else 1 - core


def side_columns(ref, side):
    return ref[:, pl.ds(pl.multiple_of(side * LANES, LANES), LANES)]


def numerator(obs, valid, counts):
    return valid.astype(F32) * counts.astype(F32) * (1.0 / COVER) * obs


def blur_pair(est_half, weight_of, spectrum_of, row_e, row_o, col_f):
    pair = jnp.concatenate([weight_of(i) * est_half for i in range(2)], axis=1)
    rows = rows_forward(row_e, row_o, pair)
    sums = None
    for i in range(2):
        fa, fb, fc, fd = to_complex(right_product(rows[:, i * LANES:(i + 1) * LANES], col_f))
        ha, hb, hc, hd = spectrum_of(i)
        terms = (fa * ha - fb * hb, fa * hb + fb * ha, fc * hc - fd * hd, fc * hd + fd * hc)
        sums = terms if sums is None else tuple(s + t for s, t in zip(sums, terms))
    return sums


def accumulate(ref, first, sums):
    if not first:
        sums = tuple(s + t for s, t in zip(load_spectrum(ref, 0), sums))
    store_spectrum(ref, 0, sums)


def blur_end(side, obs, bg, valid, counts, inv_e, inv_o, col_i, total, edge, packed, middle, window):
    plane = right_product(from_complex(*load_spectrum(total, 0)), col_i)
    window[...] = rows_inverse(inv_e, inv_o, plane, window.shape[0])
    edge[...] = side_columns(window, side)
    middle[...] = side_columns(window, 1 - side)
    num = numerator(obs, valid, counts)
    lane = lax.broadcasted_iota(jnp.int32, (1, LANES), 1)
    num = jnp.where(side == 0, num, swap(num))
    back = jnp.where(side == 0, swap(bg), bg)
    packed[...] = jnp.where(lane < LANES // 2, num, back)


def outer_blur(components, *refs):
    inputs, refs = refs[:16], refs[16:]
    (spectrum, edge, middle), refs = refs[:3], refs[3:]
    kept, refs = refs[:12], refs[12:]
    kernels, col_h, row_c, row_s, cos_columns, sin_columns, total, window, done = refs
    columns = (cos_columns, sin_columns)
    side = side_of(True)
    near = pl.ds(pl.multiple_of(side * LANES, LANES), LANES)
    far = pl.ds(pl.multiple_of((1 - side) * LANES, LANES), LANES)
    held = (kernels, col_h, row_c, row_s, *kept)
    copies = []
    for i, (ref, own) in enumerate(zip(inputs, held)):
        if i == 8:
            copies.append((ref.at[:, :, near], own.at[:, :, near]))
        else:
            copies.append((ref, own))
    copies.append((inputs[8].at[:, :, far], held[8].at[:, :, far]))
    copies = [pltpu.make_async_copy(a, b, done.at[i]) for i, (a, b) in enumerate(copies)]
    for copy in copies[:9]:
        copy.start()
    row_e, row_o, col_f, est, weights, col_i, inv_e, inv_o, obs, bg, valid, counts = kept
    size = kernels.shape[0]
    centre = size // 2
    evens, odds = row_c.shape[1] // 3, row_s.shape[1] // 3
    half = row_s.shape[0]
    copies[0].wait()
    copies[1].wait()
    above, below = kernels[centre + 1:], [kernels[i:i + 1] for i in range(centre - 1, -1, -1)]
    below = jnp.concatenate(below, axis=0)
    folded = jnp.concatenate([above - below, kernels[centre:centre + 1], above + below], axis=0)
    plane = right_product(folded.reshape(size * components, size), col_h)
    empty = (odds + evens - size) * components
    for part, ref in enumerate(columns):
        ref[:size * components] = plane[:, part * LANES:(part + 1) * LANES]
        ref[size * components:] = jnp.zeros((empty, LANES), F32)
    for copy in copies[2:9]:
        copy.wait()
    for copy in copies[9:]:
        copy.start()

    def spectrum_of(k):
        def taken(start, count):
            places = pl.ds(k + start * components, count, stride=components)
            return jnp.concatenate([ref[places, :] for ref in columns], axis=1)

        cos = left_product(row_c, taken(odds, evens))
        sin = left_product(row_s, taken(0, odds))
        sin = fix_first(cos[half:half + 1], sin)
        parts = to_complex(jnp.concatenate([cos[:half], sin], axis=0))
        store_spectrum(spectrum, k, parts)
        return parts

    for k in range(0, components, 2):
        sums = blur_pair(
            side_columns(est, side), lambda i: side_columns(weights.at[k + i], side),
            lambda i: spectrum_of(k + i), row_e, row_o, col_f,
        )
        accumulate(total, k == 0, sums)
    for copy in copies[9:]:
        copy.wait()
    tiles = (side_columns(ref, side) for ref in (obs, bg, valid, counts))
    blur_end(
        side, *tiles, inv_e, inv_o, col_i, total,
        edge.at[:, :LANES], edge.at[:, LANES:], middle, window,
    )


def inner_blur(
    est, obs, bg, valid, counts, weights, spectrum, row_e, row_o, col_f, inv_e, inv_o, col_i,
    edge, packed, middle, total, window,
):
    side = side_of(False)
    for k in range(0, weights.shape[0], 2):
        sums = blur_pair(
            side_columns(est, side), lambda i: side_columns(weights.at[k + i], side),
            lambda i: load_spectrum(spectrum, k + i), row_e, row_o, col_f,
        )
        accumulate(total, k == 0, sums)
    tiles = (side_columns(ref, side) for ref in (obs, bg, valid, counts))
    blur_end(side, *tiles, inv_e, inv_o, col_i, total, edge, packed, middle, window)


def correct_half(
    outer, est, obs, bg, sens, valid, counts, weights, spectrum, edge, received, packed, middle, other,
    row_e, row_o, col_w, inv_e, inv_o, col_i, updated, ratio, held, total, done=None,
):
    side = side_of(outer)
    lane = lax.broadcasted_iota(jnp.int32, (1, LANES), 1)
    left = lane < LANES // 2
    num = numerator(obs[...], valid[...], counts[...])

    def centre(own):
        return jnp.where(left, swap(own[:, :LANES]), swap(own[:, LANES:]))

    def at_edge(own):
        return swap(jnp.where(side == 0, own[:, :LANES], own[:, LANES:]))

    def divided(num, blurred, back):
        return jnp.where(num > 0.0, num / (blurred + back), 0.0)

    packed = packed[...]
    turned = swap(packed)
    from_other = (lane >= LANES // 2) == (side == 1)
    edge_num = jnp.where(from_other, jnp.where(side == 0, packed, turned), at_edge(num))
    edge_back = jnp.where(from_other, jnp.where(side == 0, turned, packed), at_edge(bg[...]))
    first = pl.ds(pl.multiple_of(side * LANES, LANES), LANES)
    second = pl.ds(pl.multiple_of((1 - side) * LANES, LANES), LANES)
    ratio[:, first] = divided(edge_num, edge[...] + received[...], edge_back)
    ratio[:, second] = divided(centre(num), middle[...] + other[...], centre(bg[...]))
    store_spectrum(held, 0, to_complex(right_product(rows_forward(row_e, row_o, ratio[...]), col_w)))

    for k in range(0, weights.shape[0], 2):
        planes = []
        a, b, c, d = load_spectrum(held, 0)
        for i in range(2):
            ha, hb, hc, hd = load_spectrum(spectrum, k + i)
            plane = from_complex(a * ha + b * hb, b * ha - a * hb, c * hc + d * hd, d * hc - c * hd)
            high, low = split(plane)
            both = dot(high, col_i[...])
            planes.append(both[:, :LANES] + (both[:, LANES:] + dot(low, col_i[:, :LANES])))
        pair = rows_inverse(inv_e, inv_o, jnp.concatenate(planes, axis=1), total.shape[0])
        sums = (
            side_columns(weights.at[k], side) * pair[:, :LANES]
            + side_columns(weights.at[k + 1], side) * pair[:, LANES:]
        )
        total[...] = sums if k == 0 else total[...] + sums

    result = side_columns(est, side) * total[...] / side_columns(sens, side)
    if done is None:
        updated[...] = result
    else:
        updated[:, first] = result
        updated[:, second] = done[...]


def inner_correct(*refs):
    correct_half(False, *refs)


def outer_correct(*refs):
    edge, received, middle, other, done = refs[8:13]
    correct_half(
        True, *refs[:8], edge.at[:, :LANES], received.at[:, :LANES], received.at[:, LANES:],
        middle, other, *refs[13:], done=done,
    )


def call(kernel, name, flops, args, outs, scratch, space=pltpu.VMEM):
    size = sum(a.size * a.dtype.itemsize for a in args)
    if space is pltpu.HBM:
        args = [pltpu.with_memory_space_constraint(a, pltpu.HBM) for a in args]
    return pl.pallas_call(
        kernel,
        in_specs=[pl.BlockSpec(memory_space=space)] * len(args),
        out_specs=[pl.BlockSpec(memory_space=pltpu.VMEM)] * len(outs),
        out_shape=outs,
        scratch_shapes=scratch,
        compiler_params=pltpu.CompilerParams(vmem_limit_bytes=VMEM_MIB * 2**20),
        cost_estimate=pl.CostEstimate(flops=flops // 100, bytes_accessed=size // 100, transcendentals=0),
        name=name,
    )(*args)


def local(estimate, observed, background, sensitivity, weights, kernels, valid_mask, counts):
    rows, cols = estimate.shape
    components, size = kernels.shape[0], kernels.shape[-1]
    halo = (size - 1) // 2
    half_cols = cols // 2
    row_len, col_len = rows + halo, half_cols + 2 * halo
    inner_cols = np.arange(half_cols)
    wide_cols = np.arange(-halo, half_cols + halo)
    offsets = np.arange(-halo, halo + 1)
    quarter = np.arange(row_len // 2)
    row_e, row_o = (left_table(t) for t in parity_waves(row_len, quarter))
    inv_e, inv_o = (left_table(t.T / row_len) for t in parity_waves(row_len, quarter))
    evens = -(-(halo + 1) // 16) * 16
    cos, sin = whole_waves(row_len, np.arange(halo + 1))
    cos = np.concatenate([cos, sin[:1]])
    row_c = left_table(np.pad(cos, ((0, -len(cos) % 16), (0, evens - halo - 1))))
    sin[0] = 0.0
    row_s = left_table(sin[:, 1:])
    col_h = right_table(waves(col_len, offsets).T)
    col_f = right_table(waves(col_len, inner_cols).T)
    col_w = right_table(waves(col_len, wide_cols).T)
    col_iw = right_table(waves(col_len, wide_cols) * (2.0 / col_len))
    col_i = wide_table(waves(col_len, inner_cols) * (2.0 / col_len))

    count = lax.axis_size("col")
    between = [(i, i + 1) for i in range(1, count - 1, 2)]
    between += [(j, i) for i, j in between]
    within = [(i, i ^ 1) for i in range(count)]

    macs = 3 * components * row_len * half_cols * (rows + 2 * col_len)
    plane = jax.ShapeDtypeStruct((rows, LANES), F32)
    wide = jax.ShapeDtypeStruct((rows, 2 * LANES), F32)
    spectra = jax.ShapeDtypeStruct((components, row_len, col_len), F32)
    total = pltpu.VMEM((1, row_len, col_len), F32)
    window = pltpu.VMEM((rows, col_len), F32)
    turned = jnp.transpose(kernels, (1, 0, 2))
    first = (turned, col_h, row_c, row_s)
    kept = (
        row_e, row_o, col_f, estimate, weights, col_iw, inv_e, inv_o,
        observed, background, valid_mask, counts,
    )
    columns = pltpu.VMEM(((halo + evens) * components, LANES), F32)
    spectrum, edge_o, middle_o, *kept = call(
        functools.partial(outer_blur, components), "outer_blur", 4 * macs, (*first, *kept),
        (spectra, wide, plane, *(jax.ShapeDtypeStruct(a.shape, a.dtype) for a in kept)),
        [
            *(pltpu.VMEM(a.shape, a.dtype) for a in first), columns, columns, total, window,
            pltpu.SemaphoreType.DMA((len(first) + len(kept) + 1,)),
        ],
        pltpu.HBM,
    )
    row_e, row_o, col_f, estimate, weights, col_iw, inv_e, inv_o = kept[:8]
    observed, background, valid_mask, counts = kept[8:]
    tiles = (observed, background, valid_mask, counts)
    received_o = lax.ppermute(edge_o, "col", between)
    edge_i, packed_i, middle_i = call(
        inner_blur, "inner_blur", 2 * macs,
        (estimate, *tiles, weights, spectrum, row_e, row_o, col_f, inv_e, inv_o, col_iw),
        (plane, plane, plane), [total, window],
    )
    received_i = (lax.ppermute(edge_i, "col", within), lax.ppermute(packed_i, "col", within))
    shared = (
        estimate, observed, background, sensitivity, valid_mask, counts, weights, spectrum
    )
    tables = (row_e, row_o, col_w, inv_e, inv_o, col_i)
    scratch = [window, total, pltpu.VMEM((rows, LANES), F32)]
    (half,) = call(
        inner_correct, "inner_correct", 2 * macs,
        (*shared, edge_i, *received_i, middle_i, middle_o, *tables), (plane,), scratch,
    )
    (updated,) = call(
        outer_correct, "outer_correct", 2 * macs,
        (*shared, edge_o, received_o, middle_o, middle_i, half, *tables), (wide,), scratch,
    )
    return updated


def solution(mesh):
    tile = P("group", "col")
    placed = (tile, tile, tile, tile, P(None, "group", "col"), P(), tile, tile)
    return jax.shard_map(local, mesh=mesh, in_specs=placed, out_specs=tile, check_vma=False)
```

```python
import functools

import jax
import jax.numpy as jnp
import numpy as np
from jax import lax
from jax.experimental import pallas as pl
from jax.experimental.pallas import tpu as pltpu
from jax.sharding import PartitionSpec as P

COVER = 8
LANES = 128
VMEM_MIB = 32
BF16 = jnp.bfloat16
F32 = jnp.float32


def halves(table):
    table = table.astype(np.float32)
    high = table.astype(jnp.bfloat16)
    return high, (table - high.astype(np.float32)).astype(jnp.bfloat16)


def waves(length, places):
    angles = 2.0 * np.pi * (np.arange(length // 2) + 0.5)[:, None] * np.asarray(places)[None, :] / length
    return np.concatenate([np.cos(angles), np.sin(angles)], axis=0)


def whole_waves(length, places):
    freqs = np.arange(length // 2)
    freqs = np.concatenate([freqs[0::2], freqs[1::2]])
    angles = 2.0 * np.pi * freqs[:, None] * np.asarray(places)[None, :] / length
    sin = np.sin(angles)
    sin[0] = np.cos(np.pi * np.asarray(places))
    return np.cos(angles), sin


def parity_waves(length, places):
    cos, sin = whole_waves(length, places)
    quarter = length // 4
    return (
        np.concatenate([cos[:quarter], sin[:quarter]]),
        np.concatenate([cos[quarter:], sin[quarter:]]),
    )


def left_table(table):
    high, low = halves(table)
    return jnp.asarray(np.concatenate([high, low, high], axis=1))


def right_table(table):
    high, low = halves(table)
    return jnp.asarray(np.concatenate([high, high, low], axis=0))


def wide_table(table):
    return jnp.asarray(np.concatenate(halves(table), axis=1))


def split(values):
    high = values.astype(BF16)
    return high, (values - high.astype(F32)).astype(BF16)


def dot(a, b):
    return jnp.dot(a, b, preferred_element_type=F32)


def left_product(table, values):
    high, low = split(values)
    return dot(table[...], jnp.concatenate([high, high, low], axis=0))


def right_product(values, table):
    high, low = split(values)
    return dot(jnp.concatenate([high, low, high], axis=1), table[...])


def rows_forward(even, odd, values):
    half = even.shape[1] // 3
    quarter = even.shape[0] // 2
    rest = values.shape[0] - half
    first, second, alone = values[:rest], values[half:], values[rest:half]
    e = left_product(even, jnp.concatenate([first + second, alone], axis=0))
    o = left_product(odd, jnp.concatenate([first - second, alone], axis=0))
    return jnp.concatenate([e[:quarter], o[:quarter], e[quarter:], o[quarter:]], axis=0)


def rows_inverse(even, odd, plane, rows):
    quarter = plane.shape[0] // 4
    parts = [plane[i * quarter:(i + 1) * quarter] for i in range(4)]
    e = left_product(even, jnp.concatenate([parts[0], parts[2]], axis=0))
    o = left_product(odd, jnp.concatenate([parts[1], parts[3]], axis=0))
    return jnp.concatenate([e + o, (e - o)[:rows - e.shape[0]]], axis=0)


def fix_first(first, values):
    row = lax.broadcasted_iota(jnp.int32, (8, 1), 0)
    return jnp.concatenate([jnp.where(row == 0, first, values[:8]), values[8:]], axis=0)


def to_complex(plane):
    half = plane.shape[0] // 2
    cc, cs = plane[:half, :LANES], plane[:half, LANES:]
    sc, ss = plane[half:, :LANES], plane[half:, LANES:]
    return (
        fix_first(cc[:8], cc - ss), fix_first(cs[:8], cs + sc),
        fix_first(sc[:8], cc + ss), fix_first(ss[:8], cs - sc),
    )


def from_complex(a, b, c, d):
    top = jnp.concatenate([fix_first(a[:8], a + c), fix_first(b[:8], b + d)], axis=1)
    low = jnp.concatenate([fix_first(c[:8], b - d), fix_first(d[:8], c - a)], axis=1)
    return jnp.concatenate([top, low], axis=0)


def store_spectrum(ref, index, parts):
    half = parts[0].shape[0]
    ref[index, :half, :LANES], ref[index, :half, LANES:] = parts[0], parts[1]
    ref[index, half:, :LANES], ref[index, half:, LANES:] = parts[2], parts[3]


def load_spectrum(ref, index):
    half = ref.shape[1] // 2
    return (
        ref[index, :half, :LANES], ref[index, :half, LANES:],
        ref[index, half:, :LANES], ref[index, half:, LANES:],
    )


def swap(values):
    return pltpu.roll(values, LANES // 2, 1)


def side_of(outer):
    core = lax.axis_index("col") % 2
    return core if outer else 1 - core


def side_columns(ref, side):
    return ref[:, pl.ds(pl.multiple_of(side * LANES, LANES), LANES)]


def numerator(obs, valid, counts):
    return valid.astype(F32) * counts.astype(F32) * (1.0 / COVER) * obs


def blur_pairs(est_half, weight_of, spectrum_of, components, row_e, row_o, col_f, total):
    def ahead(k):
        pair = jnp.concatenate([weight_of(k + i) * est_half for i in range(2)], axis=1)
        rows = rows_forward(row_e, row_o, pair)
        return rows, [spectrum_of(k + i) for i in range(2)]

    coming = ahead(0)
    for k in range(0, components, 2):
        rows, spectra = coming
        if k + 2 < components:
            coming = ahead(k + 2)
        sums = None
        for i in range(2):
            fa, fb, fc, fd = to_complex(right_product(rows[:, i * LANES:(i + 1) * LANES], col_f))
            ha, hb, hc, hd = spectra[i]
            terms = (fa * ha - fb * hb, fa * hb + fb * ha, fc * hc - fd * hd, fc * hd + fd * hc)
            sums = terms if sums is None else tuple(s + t for s, t in zip(sums, terms))
        accumulate(total, k == 0, sums)


def accumulate(ref, first, sums):
    if not first:
        sums = tuple(s + t for s, t in zip(load_spectrum(ref, 0), sums))
    store_spectrum(ref, 0, sums)


def blur_end(side, obs, bg, valid, counts, inv_e, inv_o, col_i, total, edge, packed, middle, window):
    plane = right_product(from_complex(*load_spectrum(total, 0)), col_i)
    window[...] = rows_inverse(inv_e, inv_o, plane, window.shape[0])
    edge[...] = side_columns(window, side)
    middle[...] = side_columns(window, 1 - side)
    num = numerator(obs, valid, counts)
    lane = lax.broadcasted_iota(jnp.int32, (1, LANES), 1)
    num = jnp.where(side == 0, num, swap(num))
    back = jnp.where(side == 0, swap(bg), bg)
    packed[...] = jnp.where(lane < LANES // 2, num, back)


def outer_blur(components, *refs):
    inputs, refs = refs[:16], refs[16:]
    (spectrum, edge, middle), refs = refs[:3], refs[3:]
    kept, refs = refs[:12], refs[12:]
    kernels, col_h, row_c, row_s, cos_columns, sin_columns, total, window, done = refs
    columns = (cos_columns, sin_columns)
    side = side_of(True)
    near = pl.ds(pl.multiple_of(side * LANES, LANES), LANES)
    far = pl.ds(pl.multiple_of((1 - side) * LANES, LANES), LANES)
    held = (kernels, col_h, row_c, row_s, *kept)
    copies = []
    for i, (ref, own) in enumerate(zip(inputs, held)):
        if i == 8:
            copies.append((ref.at[:, :, near], own.at[:, :, near]))
        else:
            copies.append((ref, own))
    copies.append((inputs[8].at[:, :, far], held[8].at[:, :, far]))
    copies = [pltpu.make_async_copy(a, b, done.at[i]) for i, (a, b) in enumerate(copies)]
    for copy in copies[:9]:
        copy.start()
    row_e, row_o, col_f, est, weights, col_i, inv_e, inv_o, obs, bg, valid, counts = kept
    size = kernels.shape[0]
    centre = size // 2
    evens, odds = row_c.shape[1] // 3, row_s.shape[1] // 3
    half = row_s.shape[0]
    copies[0].wait()
    copies[1].wait()
    above, below = kernels[centre + 1:], [kernels[i:i + 1] for i in range(centre - 1, -1, -1)]
    below = jnp.concatenate(below, axis=0)
    folded = jnp.concatenate([above - below, kernels[centre:centre + 1], above + below], axis=0)
    plane = right_product(folded.reshape(size * components, size), col_h)
    empty = (odds + evens - size) * components
    for part, ref in enumerate(columns):
        ref[:size * components] = plane[:, part * LANES:(part + 1) * LANES]
        ref[size * components:] = jnp.zeros((empty, LANES), F32)
    for copy in copies[2:9]:
        copy.wait()
    for copy in copies[9:]:
        copy.start()

    def spectrum_of(k):
        def taken(start, count):
            places = pl.ds(k + start * components, count, stride=components)
            return jnp.concatenate([ref[places, :] for ref in columns], axis=1)

        cos = left_product(row_c, taken(odds, evens))
        sin = left_product(row_s, taken(0, odds))
        sin = fix_first(cos[half:half + 1], sin)
        parts = to_complex(jnp.concatenate([cos[:half], sin], axis=0))
        store_spectrum(spectrum, k, parts)
        return parts

    blur_pairs(
        side_columns(est, side), lambda k: side_columns(weights.at[k], side), spectrum_of,
        components, row_e, row_o, col_f, total,
    )
    for copy in copies[9:]:
        copy.wait()
    tiles = (side_columns(ref, side) for ref in (obs, bg, valid, counts))
    blur_end(
        side, *tiles, inv_e, inv_o, col_i, total,
        edge.at[:, :LANES], edge.at[:, LANES:], middle, window,
    )


def inner_blur(
    est, obs, bg, valid, counts, weights, spectrum, row_e, row_o, col_f, inv_e, inv_o, col_i,
    edge, packed, middle, total, window,
):
    side = side_of(False)
    blur_pairs(
        side_columns(est, side), lambda k: side_columns(weights.at[k], side),
        lambda k: load_spectrum(spectrum, k), weights.shape[0], row_e, row_o, col_f, total,
    )
    tiles = (side_columns(ref, side) for ref in (obs, bg, valid, counts))
    blur_end(side, *tiles, inv_e, inv_o, col_i, total, edge, packed, middle, window)


def correct_half(
    outer, est, obs, bg, sens, valid, counts, weights, spectrum, edge, received, packed, middle, other,
    row_e, row_o, col_w, inv_e, inv_o, col_i, updated, ratio, held, total, done=None,
):
    side = side_of(outer)
    lane = lax.broadcasted_iota(jnp.int32, (1, LANES), 1)
    left = lane < LANES // 2
    num = numerator(obs[...], valid[...], counts[...])

    def centre(own):
        return jnp.where(left, swap(own[:, :LANES]), swap(own[:, LANES:]))

    def at_edge(own):
        return swap(jnp.where(side == 0, own[:, :LANES], own[:, LANES:]))

    def divided(num, blurred, back):
        return jnp.where(num > 0.0, num / (blurred + back), 0.0)

    packed = packed[...]
    turned = swap(packed)
    from_other = (lane >= LANES // 2) == (side == 1)
    edge_num = jnp.where(from_other, jnp.where(side == 0, packed, turned), at_edge(num))
    edge_back = jnp.where(from_other, jnp.where(side == 0, turned, packed), at_edge(bg[...]))
    first = pl.ds(pl.multiple_of(side * LANES, LANES), LANES)
    second = pl.ds(pl.multiple_of((1 - side) * LANES, LANES), LANES)
    ratio[:, first] = divided(edge_num, edge[...] + received[...], edge_back)
    ratio[:, second] = divided(centre(num), middle[...] + other[...], centre(bg[...]))
    store_spectrum(held, 0, to_complex(right_product(rows_forward(row_e, row_o, ratio[...]), col_w)))

    def filtered(k):
        planes = []
        a, b, c, d = load_spectrum(held, 0)
        for i in range(2):
            ha, hb, hc, hd = load_spectrum(spectrum, k + i)
            plane = from_complex(a * ha + b * hb, b * ha - a * hb, c * hc + d * hd, d * hc - c * hd)
            high, low = split(plane)
            both = dot(high, col_i[...])
            planes.append(both[:, :LANES] + (both[:, LANES:] + dot(low, col_i[:, :LANES])))
        return jnp.concatenate(planes, axis=1)

    components = weights.shape[0]
    ahead = filtered(0)
    for k in range(0, components, 2):
        planes = ahead
        if k + 2 < components:
            ahead = filtered(k + 2)
        pair = rows_inverse(inv_e, inv_o, planes, total.shape[0])
        sums = (
            side_columns(weights.at[k], side) * pair[:, :LANES]
            + side_columns(weights.at[k + 1], side) * pair[:, LANES:]
        )
        total[...] = sums if k == 0 else total[...] + sums

    result = side_columns(est, side) * total[...] / side_columns(sens, side)
    if done is None:
        updated[...] = result
    else:
        updated[:, first] = result
        updated[:, second] = done[...]


def inner_correct(*refs):
    correct_half(False, *refs)


def outer_correct(*refs):
    edge, received, middle, other, done = refs[8:13]
    correct_half(
        True, *refs[:8], edge.at[:, :LANES], received.at[:, :LANES], received.at[:, LANES:],
        middle, other, *refs[13:], done=done,
    )


def call(kernel, name, flops, args, outs, scratch, space=pltpu.VMEM):
    size = sum(a.size * a.dtype.itemsize for a in args)
    if space is pltpu.HBM:
        args = [pltpu.with_memory_space_constraint(a, pltpu.HBM) for a in args]
    return pl.pallas_call(
        kernel,
        in_specs=[pl.BlockSpec(memory_space=space)] * len(args),
        out_specs=[pl.BlockSpec(memory_space=pltpu.VMEM)] * len(outs),
        out_shape=outs,
        scratch_shapes=scratch,
        compiler_params=pltpu.CompilerParams(vmem_limit_bytes=VMEM_MIB * 2**20),
        cost_estimate=pl.CostEstimate(flops=flops // 100, bytes_accessed=size // 100, transcendentals=0),
        name=name,
    )(*args)


def local(estimate, observed, background, sensitivity, weights, kernels, valid_mask, counts):
    rows, cols = estimate.shape
    components, size = kernels.shape[0], kernels.shape[-1]
    halo = (size - 1) // 2
    half_cols = cols // 2
    row_len, col_len = rows + halo, half_cols + 2 * halo
    inner_cols = np.arange(half_cols)
    wide_cols = np.arange(-halo, half_cols + halo)
    offsets = np.arange(-halo, halo + 1)
    quarter = np.arange(row_len // 2)
    row_e, row_o = (left_table(t) for t in parity_waves(row_len, quarter))
    inv_e, inv_o = (left_table(t.T / row_len) for t in parity_waves(row_len, quarter))
    evens = -(-(halo + 1) // 16) * 16
    cos, sin = whole_waves(row_len, np.arange(halo + 1))
    cos = np.concatenate([cos, sin[:1]])
    row_c = left_table(np.pad(cos, ((0, -len(cos) % 16), (0, evens - halo - 1))))
    sin[0] = 0.0
    row_s = left_table(sin[:, 1:])
    col_h = right_table(waves(col_len, offsets).T)
    col_f = right_table(waves(col_len, inner_cols).T)
    col_w = right_table(waves(col_len, wide_cols).T)
    col_iw = right_table(waves(col_len, wide_cols) * (2.0 / col_len))
    col_i = wide_table(waves(col_len, inner_cols) * (2.0 / col_len))

    count = lax.axis_size("col")
    between = [(i, i + 1) for i in range(1, count - 1, 2)]
    between += [(j, i) for i, j in between]
    within = [(i, i ^ 1) for i in range(count)]

    macs = 3 * components * row_len * half_cols * (rows + 2 * col_len)
    plane = jax.ShapeDtypeStruct((rows, LANES), F32)
    wide = jax.ShapeDtypeStruct((rows, 2 * LANES), F32)
    spectra = jax.ShapeDtypeStruct((components, row_len, col_len), F32)
    total = pltpu.VMEM((1, row_len, col_len), F32)
    window = pltpu.VMEM((rows, col_len), F32)
    turned = jnp.transpose(kernels, (1, 0, 2))
    first = (turned, col_h, row_c, row_s)
    kept = (
        row_e, row_o, col_f, estimate, weights, col_iw, inv_e, inv_o,
        observed, background, valid_mask, counts,
    )
    columns = pltpu.VMEM(((halo + evens) * components, LANES), F32)
    spectrum, edge_o, middle_o, *kept = call(
        functools.partial(outer_blur, components), "outer_blur", 4 * macs, (*first, *kept),
        (spectra, wide, plane, *(jax.ShapeDtypeStruct(a.shape, a.dtype) for a in kept)),
        [
            *(pltpu.VMEM(a.shape, a.dtype) for a in first), columns, columns, total, window,
            pltpu.SemaphoreType.DMA((len(first) + len(kept) + 1,)),
        ],
        pltpu.HBM,
    )
    row_e, row_o, col_f, estimate, weights, col_iw, inv_e, inv_o = kept[:8]
    observed, background, valid_mask, counts = kept[8:]
    tiles = (observed, background, valid_mask, counts)
    received_o = lax.ppermute(edge_o, "col", between)
    edge_i, packed_i, middle_i = call(
        inner_blur, "inner_blur", 2 * macs,
        (estimate, *tiles, weights, spectrum, row_e, row_o, col_f, inv_e, inv_o, col_iw),
        (plane, plane, plane), [total, window],
    )
    received_i = (lax.ppermute(edge_i, "col", within), lax.ppermute(packed_i, "col", within))
    shared = (
        estimate, observed, background, sensitivity, valid_mask, counts, weights, spectrum
    )
    tables = (row_e, row_o, col_w, inv_e, inv_o, col_i)
    scratch = [window, total, pltpu.VMEM((rows, LANES), F32)]
    (half,) = call(
        inner_correct, "inner_correct", 2 * macs,
        (*shared, edge_i, *received_i, middle_i, middle_o, *tables), (plane,), scratch,
    )
    (updated,) = call(
        outer_correct, "outer_correct", 2 * macs,
        (*shared, edge_o, received_o, middle_o, middle_i, half, *tables), (wide,), scratch,
    )
    return updated


def solution(mesh):
    tile = P("group", "col")
    placed = (tile, tile, tile, tile, P(None, "group", "col"), P(), tile, tile)
    return jax.shard_map(local, mesh=mesh, in_specs=placed, out_specs=tile, check_vma=False)
```

```python
import functools

import jax
import jax.numpy as jnp
import numpy as np
from jax import lax
from jax.experimental import pallas as pl
from jax.experimental.pallas import tpu as pltpu
from jax.sharding import PartitionSpec as P

COVER = 8
LANES = 128
VMEM_MIB = 32
CHUNKS = 2
BF16 = jnp.bfloat16
F32 = jnp.float32


def halves(table):
    table = table.astype(np.float32)
    high = table.astype(jnp.bfloat16)
    return high, (table - high.astype(np.float32)).astype(jnp.bfloat16)


def waves(length, places):
    angles = 2.0 * np.pi * (np.arange(length // 2) + 0.5)[:, None] * np.asarray(places)[None, :] / length
    return np.concatenate([np.cos(angles), np.sin(angles)], axis=0)


def whole_waves(length, places):
    freqs = np.arange(length // 2)
    freqs = np.concatenate([freqs[0::2], freqs[1::2]])
    angles = 2.0 * np.pi * freqs[:, None] * np.asarray(places)[None, :] / length
    sin = np.sin(angles)
    sin[0] = np.cos(np.pi * np.asarray(places))
    return np.cos(angles), sin


def parity_waves(length, places):
    cos, sin = whole_waves(length, places)
    quarter = length // 4
    return (
        np.concatenate([cos[:quarter], sin[:quarter]]),
        np.concatenate([cos[quarter:], sin[quarter:]]),
    )


def left_table(table):
    high, low = halves(table)
    return jnp.asarray(np.concatenate([high, low, high], axis=1))


def right_table(table):
    high, low = halves(table)
    return jnp.asarray(np.concatenate([high, high, low], axis=0))


def wide_table(table):
    return jnp.asarray(np.concatenate(halves(table), axis=1))


def split(values):
    high = values.astype(BF16)
    return high, (values - high.astype(F32)).astype(BF16)


def dot(a, b):
    return jnp.dot(a, b, preferred_element_type=F32)


def left_product(table, values):
    high, low = split(values)
    return dot(table[...], jnp.concatenate([high, high, low], axis=0))


def right_product(values, table):
    high, low = split(values)
    return dot(jnp.concatenate([high, low, high], axis=1), table[...])


def rows_forward(even, odd, values):
    half = even.shape[1] // 3
    quarter = even.shape[0] // 2
    rest = values.shape[0] - half
    first, second, alone = values[:rest], values[half:], values[rest:half]
    e = left_product(even, jnp.concatenate([first + second, alone], axis=0))
    o = left_product(odd, jnp.concatenate([first - second, alone], axis=0))
    return jnp.concatenate([e[:quarter], o[:quarter], e[quarter:], o[quarter:]], axis=0)


def rows_inverse(even, odd, plane, rows):
    quarter = plane.shape[0] // 4
    parts = [plane[i * quarter:(i + 1) * quarter] for i in range(4)]
    e = left_product(even, jnp.concatenate([parts[0], parts[2]], axis=0))
    o = left_product(odd, jnp.concatenate([parts[1], parts[3]], axis=0))
    return jnp.concatenate([e + o, (e - o)[:rows - e.shape[0]]], axis=0)


def fix_first(first, values):
    row = lax.broadcasted_iota(jnp.int32, (8, 1), 0)
    return jnp.concatenate([jnp.where(row == 0, first, values[:8]), values[8:]], axis=0)


def to_complex(plane):
    half = plane.shape[0] // 2
    cc, cs = plane[:half, :LANES], plane[:half, LANES:]
    sc, ss = plane[half:, :LANES], plane[half:, LANES:]
    return (
        fix_first(cc[:8], cc - ss), fix_first(cs[:8], cs + sc),
        fix_first(sc[:8], cc + ss), fix_first(ss[:8], cs - sc),
    )


def from_complex(a, b, c, d):
    top = jnp.concatenate([fix_first(a[:8], a + c), fix_first(b[:8], b + d)], axis=1)
    low = jnp.concatenate([fix_first(c[:8], b - d), fix_first(d[:8], c - a)], axis=1)
    return jnp.concatenate([top, low], axis=0)


def store_spectrum(ref, index, parts):
    half = parts[0].shape[0]
    ref[index, :half, :LANES], ref[index, :half, LANES:] = parts[0], parts[1]
    ref[index, half:, :LANES], ref[index, half:, LANES:] = parts[2], parts[3]


def load_spectrum(ref, index):
    half = ref.shape[1] // 2
    return (
        ref[index, :half, :LANES], ref[index, :half, LANES:],
        ref[index, half:, :LANES], ref[index, half:, LANES:],
    )


def swap(values):
    return pltpu.roll(values, LANES // 2, 1)


def side_of(outer):
    core = lax.axis_index("col") % 2
    return core if outer else 1 - core


def side_columns(ref, side):
    return ref[:, pl.ds(pl.multiple_of(side * LANES, LANES), LANES)]


def numerator(obs, valid, counts):
    return valid.astype(F32) * counts.astype(F32) * (1.0 / COVER) * obs


def blur_pairs(est_half, weight_of, spectrum_of, components, row_e, row_o, col_f, total):
    def ahead(k):
        pair = jnp.concatenate([weight_of(k + i) * est_half for i in range(2)], axis=1)
        rows = rows_forward(row_e, row_o, pair)
        return rows, [spectrum_of(k + i) for i in range(2)]

    coming = ahead(0)
    for k in range(0, components, 2):
        rows, spectra = coming
        if k + 2 < components:
            coming = ahead(k + 2)
        sums = None
        for i in range(2):
            fa, fb, fc, fd = to_complex(right_product(rows[:, i * LANES:(i + 1) * LANES], col_f))
            ha, hb, hc, hd = spectra[i]
            terms = (fa * ha - fb * hb, fa * hb + fb * ha, fc * hc - fd * hd, fc * hd + fd * hc)
            sums = terms if sums is None else tuple(s + t for s, t in zip(sums, terms))
        accumulate(total, k == 0, sums)


def accumulate(ref, first, sums):
    if not first:
        sums = tuple(s + t for s, t in zip(load_spectrum(ref, 0), sums))
    store_spectrum(ref, 0, sums)


def blur_end(side, obs, bg, valid, counts, inv_e, inv_o, col_i, total, edge, packed, middle, window):
    plane = rows_inverse(inv_e, inv_o, from_complex(*load_spectrum(total, 0)), window.shape[0])
    window[...] = right_product(plane, col_i)
    edge[...] = side_columns(window, side)
    middle[...] = side_columns(window, 1 - side)
    num = numerator(obs, valid, counts)
    lane = lax.broadcasted_iota(jnp.int32, (1, LANES), 1)
    num = jnp.where(side == 0, num, swap(num))
    back = jnp.where(side == 0, swap(bg), bg)
    packed[...] = jnp.where(lane < LANES // 2, num, back)


def outer_blur(components, *refs):
    inputs, refs = refs[:16], refs[16:]
    (spectrum, edge, middle), refs = refs[:3], refs[3:]
    kept, refs = refs[:12], refs[12:]
    kernels, col_h, row_c, row_s, cos_columns, sin_columns, total, window, done = refs
    columns = (cos_columns, sin_columns)
    side = side_of(True)
    near = pl.ds(pl.multiple_of(side * LANES, LANES), LANES)
    far = pl.ds(pl.multiple_of((1 - side) * LANES, LANES), LANES)
    held = (kernels, col_h, row_c, row_s, *kept)
    copies = []
    for i, (ref, own) in enumerate(zip(inputs, held)):
        if i == 8:
            copies.append((ref.at[:, :, near], own.at[:, :, near]))
        else:
            copies.append((ref, own))
    copies.append((inputs[8].at[:, :, far], held[8].at[:, :, far]))
    copies = [pltpu.make_async_copy(a, b, done.at[i]) for i, (a, b) in enumerate(copies)]
    for copy in copies[:9]:
        copy.start()
    row_e, row_o, col_f, est, weights, col_i, inv_e, inv_o, obs, bg, valid, counts = kept
    size = kernels.shape[0]
    centre = size // 2
    evens, odds = row_c.shape[1] // 3, row_s.shape[1] // 3
    half = row_s.shape[0]
    copies[0].wait()
    copies[1].wait()
    above, below = kernels[centre + 1:], [kernels[i:i + 1] for i in range(centre - 1, -1, -1)]
    below = jnp.concatenate(below, axis=0)
    folded = jnp.concatenate([above - below, kernels[centre:centre + 1], above + below], axis=0)
    plane = right_product(folded.reshape(size * components, size), col_h)
    empty = (odds + evens - size) * components
    for part, ref in enumerate(columns):
        ref[:size * components] = plane[:, part * LANES:(part + 1) * LANES]
        ref[size * components:] = jnp.zeros((empty, LANES), F32)
    for copy in copies[2:9]:
        copy.wait()
    for copy in copies[9:]:
        copy.start()

    def spectrum_of(k):
        def taken(start, count):
            places = pl.ds(k + start * components, count, stride=components)
            return jnp.concatenate([ref[places, :] for ref in columns], axis=1)

        cos = left_product(row_c, taken(odds, evens))
        sin = left_product(row_s, taken(0, odds))
        sin = fix_first(cos[half:half + 1], sin)
        parts = to_complex(jnp.concatenate([cos[:half], sin], axis=0))
        store_spectrum(spectrum, k, parts)
        return parts

    blur_pairs(
        side_columns(est, side), lambda k: side_columns(weights.at[k], side), spectrum_of,
        components, row_e, row_o, col_f, total,
    )
    for copy in copies[9:]:
        copy.wait()
    tiles = (side_columns(ref, side) for ref in (obs, bg, valid, counts))
    blur_end(
        side, *tiles, inv_e, inv_o, col_i, total,
        edge.at[:, :LANES], edge.at[:, LANES:], middle, window,
    )


def inner_blur(
    est, obs, bg, valid, counts, weights, spectrum, row_e, row_o, col_f, inv_e, inv_o, col_i,
    edge, packed, middle, total, window,
):
    side = side_of(False)
    blur_pairs(
        side_columns(est, side), lambda k: side_columns(weights.at[k], side),
        lambda k: load_spectrum(spectrum, k), weights.shape[0], row_e, row_o, col_f, total,
    )
    tiles = (side_columns(ref, side) for ref in (obs, bg, valid, counts))
    blur_end(side, *tiles, inv_e, inv_o, col_i, total, edge, packed, middle, window)


def correct_half(
    outer, est, obs, bg, sens, valid, counts, weights, spectrum, edge, received, packed, middle, other,
    row_e, row_o, col_w, inv_e, inv_o, col_i, updated, ratio, held, total, done=None,
):
    side = side_of(outer)
    lane = lax.broadcasted_iota(jnp.int32, (1, LANES), 1)
    left = lane < LANES // 2
    from_other = (lane >= LANES // 2) == (side == 1)

    def divided(num, blurred, back):
        return jnp.where(num > 0.0, num / (blurred + back), 0.0)

    first = pl.ds(pl.multiple_of(side * LANES, LANES), LANES)
    second = pl.ds(pl.multiple_of((1 - side) * LANES, LANES), LANES)
    count = obs.shape[0] // CHUNKS
    pieces = []
    for start in range(0, obs.shape[0], count):
        some = slice(start, start + count)
        num, back = numerator(obs[some], valid[some], counts[some]), bg[some]

        def centre(own):
            return jnp.where(left, swap(own[:, :LANES]), swap(own[:, LANES:]))

        def at_edge(own):
            return swap(jnp.where(side == 0, own[:, :LANES], own[:, LANES:]))

        straight = packed[some]
        turned = swap(straight)
        edge_num = jnp.where(from_other, jnp.where(side == 0, straight, turned), at_edge(num))
        edge_back = jnp.where(from_other, jnp.where(side == 0, turned, straight), at_edge(back))
        ratio[some, first] = divided(edge_num, edge[some] + received[some], edge_back)
        ratio[some, second] = divided(centre(num), middle[some] + other[some], centre(back))
        pieces.append(right_product(ratio[some], col_w))
    turned_ratio = jnp.concatenate(pieces, axis=0)
    store_spectrum(held, 0, to_complex(rows_forward(row_e, row_o, turned_ratio)))

    def filtered(k):
        planes = []
        a, b, c, d = load_spectrum(held, 0)
        for i in range(2):
            ha, hb, hc, hd = load_spectrum(spectrum, k + i)
            plane = from_complex(a * ha + b * hb, b * ha - a * hb, c * hc + d * hd, d * hc - c * hd)
            high, low = split(plane)
            both = dot(high, col_i[...])
            planes.append(both[:, :LANES] + (both[:, LANES:] + dot(low, col_i[:, :LANES])))
        return jnp.concatenate(planes, axis=1)

    components = weights.shape[0]
    ahead = filtered(0)
    for k in range(0, components, 2):
        planes = ahead
        if k + 2 < components:
            ahead = filtered(k + 2)
        pair = rows_inverse(inv_e, inv_o, planes, total.shape[0])
        sums = (
            side_columns(weights.at[k], side) * pair[:, :LANES]
            + side_columns(weights.at[k + 1], side) * pair[:, LANES:]
        )
        total[...] = sums if k == 0 else total[...] + sums

    result = side_columns(est, side) * total[...] / side_columns(sens, side)
    if done is None:
        updated[...] = result
    else:
        updated[:, first] = result
        updated[:, second] = done[...]


def inner_correct(*refs):
    correct_half(False, *refs)


def outer_correct(*refs):
    edge, received, middle, other, done = refs[8:13]
    correct_half(
        True, *refs[:8], edge.at[:, :LANES], received.at[:, :LANES], received.at[:, LANES:],
        middle, other, *refs[13:], done=done,
    )


def call(kernel, name, flops, args, outs, scratch, space=pltpu.VMEM):
    size = sum(a.size * a.dtype.itemsize for a in args)
    if space is pltpu.HBM:
        args = [pltpu.with_memory_space_constraint(a, pltpu.HBM) for a in args]
    return pl.pallas_call(
        kernel,
        in_specs=[pl.BlockSpec(memory_space=space)] * len(args),
        out_specs=[pl.BlockSpec(memory_space=pltpu.VMEM)] * len(outs),
        out_shape=outs,
        scratch_shapes=scratch,
        compiler_params=pltpu.CompilerParams(vmem_limit_bytes=VMEM_MIB * 2**20),
        cost_estimate=pl.CostEstimate(flops=flops // 100, bytes_accessed=size // 100, transcendentals=0),
        name=name,
    )(*args)


def local(estimate, observed, background, sensitivity, weights, kernels, valid_mask, counts):
    rows, cols = estimate.shape
    components, size = kernels.shape[0], kernels.shape[-1]
    halo = (size - 1) // 2
    half_cols = cols // 2
    row_len, col_len = rows + halo, half_cols + 2 * halo
    inner_cols = np.arange(half_cols)
    wide_cols = np.arange(-halo, half_cols + halo)
    offsets = np.arange(-halo, halo + 1)
    quarter = np.arange(row_len // 2)
    row_e, row_o = (left_table(t) for t in parity_waves(row_len, quarter))
    inv_e, inv_o = (left_table(t.T / row_len) for t in parity_waves(row_len, quarter))
    evens = -(-(halo + 1) // 16) * 16
    cos, sin = whole_waves(row_len, np.arange(halo + 1))
    cos = np.concatenate([cos, sin[:1]])
    row_c = left_table(np.pad(cos, ((0, -len(cos) % 16), (0, evens - halo - 1))))
    sin[0] = 0.0
    row_s = left_table(sin[:, 1:])
    col_h = right_table(waves(col_len, offsets).T)
    col_f = right_table(waves(col_len, inner_cols).T)
    col_w = right_table(waves(col_len, wide_cols).T)
    col_iw = right_table(waves(col_len, wide_cols) * (2.0 / col_len))
    col_i = wide_table(waves(col_len, inner_cols) * (2.0 / col_len))

    count = lax.axis_size("col")
    between = [(i, i + 1) for i in range(1, count - 1, 2)]
    between += [(j, i) for i, j in between]
    within = [(i, i ^ 1) for i in range(count)]

    macs = 3 * components * row_len * half_cols * (rows + 2 * col_len)
    plane = jax.ShapeDtypeStruct((rows, LANES), F32)
    wide = jax.ShapeDtypeStruct((rows, 2 * LANES), F32)
    spectra = jax.ShapeDtypeStruct((components, row_len, col_len), F32)
    total = pltpu.VMEM((1, row_len, col_len), F32)
    window = pltpu.VMEM((rows, col_len), F32)
    turned = jnp.transpose(kernels, (1, 0, 2))
    first = (turned, col_h, row_c, row_s)
    kept = (
        row_e, row_o, col_f, estimate, weights, col_iw, inv_e, inv_o,
        observed, background, valid_mask, counts,
    )
    columns = pltpu.VMEM(((halo + evens) * components, LANES), F32)
    spectrum, edge_o, middle_o, *kept = call(
        functools.partial(outer_blur, components), "outer_blur", 4 * macs, (*first, *kept),
        (spectra, wide, plane, *(jax.ShapeDtypeStruct(a.shape, a.dtype) for a in kept)),
        [
            *(pltpu.VMEM(a.shape, a.dtype) for a in first), columns, columns, total, window,
            pltpu.SemaphoreType.DMA((len(first) + len(kept) + 1,)),
        ],
        pltpu.HBM,
    )
    row_e, row_o, col_f, estimate, weights, col_iw, inv_e, inv_o = kept[:8]
    observed, background, valid_mask, counts = kept[8:]
    tiles = (observed, background, valid_mask, counts)
    received_o = lax.ppermute(edge_o, "col", between)
    edge_i, packed_i, middle_i = call(
        inner_blur, "inner_blur", 2 * macs,
        (estimate, *tiles, weights, spectrum, row_e, row_o, col_f, inv_e, inv_o, col_iw),
        (plane, plane, plane), [total, window],
    )
    received_i = (lax.ppermute(edge_i, "col", within), lax.ppermute(packed_i, "col", within))
    shared = (
        estimate, observed, background, sensitivity, valid_mask, counts, weights, spectrum
    )
    tables = (row_e, row_o, col_w, inv_e, inv_o, col_i)
    scratch = [window, total, pltpu.VMEM((rows, LANES), F32)]
    (half,) = call(
        inner_correct, "inner_correct", 2 * macs,
        (*shared, edge_i, *received_i, middle_i, middle_o, *tables), (plane,), scratch,
    )
    (updated,) = call(
        outer_correct, "outer_correct", 2 * macs,
        (*shared, edge_o, received_o, middle_o, middle_i, half, *tables), (wide,), scratch,
    )
    return updated


def solution(mesh):
    tile = P("group", "col")
    placed = (tile, tile, tile, tile, P(None, "group", "col"), P(), tile, tile)
    return jax.shard_map(local, mesh=mesh, in_specs=placed, out_specs=tile, check_vma=False)
```

```python
import functools

import jax
import jax.numpy as jnp
import numpy as np
from jax import lax
from jax.experimental import pallas as pl
from jax.experimental.pallas import tpu as pltpu
from jax.sharding import PartitionSpec as P

COVER = 8
LANES = 128
VMEM_MIB = 32
CHUNKS = 2
BF16 = jnp.bfloat16
F32 = jnp.float32


def halves(table):
    table = table.astype(np.float32)
    high = table.astype(jnp.bfloat16)
    return high, (table - high.astype(np.float32)).astype(jnp.bfloat16)


def waves(length, places):
    angles = 2.0 * np.pi * (np.arange(length // 2) + 0.5)[:, None] * np.asarray(places)[None, :] / length
    return np.concatenate([np.cos(angles), np.sin(angles)], axis=0)


def whole_waves(length, places):
    freqs = np.arange(length // 2)
    freqs = np.concatenate([freqs[0::2], freqs[1::2]])
    angles = 2.0 * np.pi * freqs[:, None] * np.asarray(places)[None, :] / length
    sin = np.sin(angles)
    sin[0] = np.cos(np.pi * np.asarray(places))
    return np.cos(angles), sin


def parity_waves(length, places):
    cos, sin = whole_waves(length, places)
    quarter = length // 4
    return (
        np.concatenate([cos[:quarter], sin[:quarter]]),
        np.concatenate([cos[quarter:], sin[quarter:]]),
    )


def left_table(table):
    high, low = halves(table)
    return jnp.asarray(np.concatenate([high, low, high], axis=1))


def right_table(table):
    high, low = halves(table)
    return jnp.asarray(np.concatenate([high, high, low], axis=0))


def wide_table(table):
    return jnp.asarray(np.concatenate(halves(table), axis=1))


def split(values):
    high = values.astype(BF16)
    return high, (values - high.astype(F32)).astype(BF16)


def dot(a, b):
    return jnp.dot(a, b, preferred_element_type=F32)


def left_product(table, values):
    high, low = split(values)
    return dot(table[...], jnp.concatenate([high, high, low], axis=0))


def right_product(values, table):
    high, low = split(values)
    return dot(jnp.concatenate([high, low, high], axis=1), table[...])


def rows_forward(even, odd, values):
    half = even.shape[1] // 3
    quarter = even.shape[0] // 2
    rest = values.shape[0] - half
    first, second, alone = values[:rest], values[half:], values[rest:half]
    e = left_product(even, jnp.concatenate([first + second, alone], axis=0))
    o = left_product(odd, jnp.concatenate([first - second, alone], axis=0))
    return jnp.concatenate([e[:quarter], o[:quarter], e[quarter:], o[quarter:]], axis=0)


def rows_inverse(even, odd, plane, rows):
    quarter = plane.shape[0] // 4
    parts = [plane[i * quarter:(i + 1) * quarter] for i in range(4)]
    e = left_product(even, jnp.concatenate([parts[0], parts[2]], axis=0))
    o = left_product(odd, jnp.concatenate([parts[1], parts[3]], axis=0))
    return jnp.concatenate([e + o, (e - o)[:rows - e.shape[0]]], axis=0)


def fix_first(first, values):
    row = lax.broadcasted_iota(jnp.int32, (8, 1), 0)
    return jnp.concatenate([jnp.where(row == 0, first, values[:8]), values[8:]], axis=0)


def to_complex(plane):
    half = plane.shape[0] // 2
    cc, cs = plane[:half, :LANES], plane[:half, LANES:]
    sc, ss = plane[half:, :LANES], plane[half:, LANES:]
    return (
        fix_first(cc[:8], cc - ss), fix_first(cs[:8], cs + sc),
        fix_first(sc[:8], cc + ss), fix_first(ss[:8], cs - sc),
    )


def from_complex(a, b, c, d):
    top = jnp.concatenate([fix_first(a[:8], a + c), fix_first(b[:8], b + d)], axis=1)
    low = jnp.concatenate([fix_first(c[:8], b - d), fix_first(d[:8], c - a)], axis=1)
    return jnp.concatenate([top, low], axis=0)


def store_spectrum(ref, index, parts):
    half = parts[0].shape[0]
    ref[index, :half, :LANES], ref[index, :half, LANES:] = parts[0], parts[1]
    ref[index, half:, :LANES], ref[index, half:, LANES:] = parts[2], parts[3]


def load_spectrum(ref, index):
    half = ref.shape[1] // 2
    return (
        ref[index, :half, :LANES], ref[index, :half, LANES:],
        ref[index, half:, :LANES], ref[index, half:, LANES:],
    )


def swap(values):
    return pltpu.roll(values, LANES // 2, 1)


def side_of(outer):
    core = lax.axis_index("col") % 2
    return core if outer else 1 - core


def side_columns(ref, side):
    return ref[:, pl.ds(pl.multiple_of(side * LANES, LANES), LANES)]


def numerator(obs, valid, counts):
    return valid.astype(F32) * counts.astype(F32) * (1.0 / COVER) * obs


def blur_pairs(est_half, weight_of, spectrum_of, components, row_e, row_o, col_f, total):
    def ahead(k):
        pair = jnp.concatenate([weight_of(k + i) * est_half for i in range(2)], axis=1)
        spectra = [spectrum_of(k + i) for i in range(2)]
        return rows_forward(row_e, row_o, pair), spectra

    coming = ahead(0)
    for k in range(0, components, 2):
        rows, spectra = coming
        if k + 2 < components:
            coming = ahead(k + 2)
        sums = None
        for i in range(2):
            fa, fb, fc, fd = to_complex(right_product(rows[:, i * LANES:(i + 1) * LANES], col_f))
            ha, hb, hc, hd = spectra[i]
            terms = (fa * ha - fb * hb, fa * hb + fb * ha, fc * hc - fd * hd, fc * hd + fd * hc)
            sums = terms if sums is None else tuple(s + t for s, t in zip(sums, terms))
        accumulate(total, k == 0, sums)


def accumulate(ref, first, sums):
    if not first:
        sums = tuple(s + t for s, t in zip(load_spectrum(ref, 0), sums))
    store_spectrum(ref, 0, sums)


def blur_end(side, obs, bg, valid, counts, inv_e, inv_o, col_i, total, edge, packed, middle, window):
    plane = rows_inverse(inv_e, inv_o, from_complex(*load_spectrum(total, 0)), window.shape[0])
    window[...] = right_product(plane, col_i)
    edge[...] = side_columns(window, side)
    middle[...] = side_columns(window, 1 - side)
    num = numerator(obs, valid, counts)
    lane = lax.broadcasted_iota(jnp.int32, (1, LANES), 1)
    num = jnp.where(side == 0, num, swap(num))
    back = jnp.where(side == 0, swap(bg), bg)
    packed[...] = jnp.where(lane < LANES // 2, num, back)


def outer_blur(components, *refs):
    inputs, refs = refs[:16], refs[16:]
    (spectrum, edge, middle), refs = refs[:3], refs[3:]
    kept, refs = refs[:12], refs[12:]
    kernels, col_h, row_c, row_s, cos_columns, sin_columns, total, window, done = refs
    columns = (cos_columns, sin_columns)
    side = side_of(True)
    near = pl.ds(pl.multiple_of(side * LANES, LANES), LANES)
    far = pl.ds(pl.multiple_of((1 - side) * LANES, LANES), LANES)
    held = (kernels, col_h, row_c, row_s, *kept)
    copies = []
    for i, (ref, own) in enumerate(zip(inputs, held)):
        if i == 8:
            copies.append((ref.at[:, :, near], own.at[:, :, near]))
        else:
            copies.append((ref, own))
    copies.append((inputs[8].at[:, :, far], held[8].at[:, :, far]))
    copies = [pltpu.make_async_copy(a, b, done.at[i]) for i, (a, b) in enumerate(copies)]
    for copy in copies[:9]:
        copy.start()
    row_e, row_o, col_f, est, weights, col_i, inv_e, inv_o, obs, bg, valid, counts = kept
    size = kernels.shape[0]
    centre = size // 2
    evens, odds = row_c.shape[1] // 3, row_s.shape[1] // 3
    half = row_s.shape[0]
    copies[0].wait()
    copies[1].wait()
    above, below = kernels[centre + 1:], [kernels[i:i + 1] for i in range(centre - 1, -1, -1)]
    below = jnp.concatenate(below, axis=0)
    turned = (above - below, jnp.concatenate([kernels[centre:centre + 1], above + below], axis=0))
    start = 0
    for folded in turned:
        flat = folded.reshape(-1, size)
        plane = right_product(flat, col_h)
        for part, ref in enumerate(columns):
            ref[start:start + len(flat)] = plane[:, part * LANES:(part + 1) * LANES]
        start += len(flat)
    empty = (odds + evens - size) * components
    for ref in columns:
        ref[start:] = jnp.zeros((empty, LANES), F32)
    for copy in copies[2:9]:
        copy.wait()
    for copy in copies[9:]:
        copy.start()

    def spectrum_of(k):
        def taken(start, count):
            places = pl.ds(k + start * components, count, stride=components)
            return jnp.concatenate([ref[places, :] for ref in columns], axis=1)

        cos = left_product(row_c, taken(odds, evens))
        sin = left_product(row_s, taken(0, odds))
        sin = fix_first(cos[half:half + 1], sin)
        parts = to_complex(jnp.concatenate([cos[:half], sin], axis=0))
        store_spectrum(spectrum, k, parts)
        return parts

    blur_pairs(
        side_columns(est, side), lambda k: side_columns(weights.at[k], side), spectrum_of,
        components, row_e, row_o, col_f, total,
    )
    for copy in copies[9:]:
        copy.wait()
    tiles = (side_columns(ref, side) for ref in (obs, bg, valid, counts))
    blur_end(
        side, *tiles, inv_e, inv_o, col_i, total,
        edge.at[:, :LANES], edge.at[:, LANES:], middle, window,
    )


def inner_blur(
    est, obs, bg, valid, counts, weights, spectrum, row_e, row_o, col_f, inv_e, inv_o, col_i,
    edge, packed, middle, total, window,
):
    side = side_of(False)
    blur_pairs(
        side_columns(est, side), lambda k: side_columns(weights.at[k], side),
        lambda k: load_spectrum(spectrum, k), weights.shape[0], row_e, row_o, col_f, total,
    )
    tiles = (side_columns(ref, side) for ref in (obs, bg, valid, counts))
    blur_end(side, *tiles, inv_e, inv_o, col_i, total, edge, packed, middle, window)


def correct_half(
    outer, est, obs, bg, sens, valid, counts, weights, spectrum, edge, received, packed, middle, other,
    row_e, row_o, col_w, inv_e, inv_o, col_i, updated, ratio, held, total, done=None,
):
    side = side_of(outer)
    lane = lax.broadcasted_iota(jnp.int32, (1, LANES), 1)
    left = lane < LANES // 2
    from_other = (lane >= LANES // 2) == (side == 1)

    def divided(num, blurred, back):
        return jnp.where(num > 0.0, num / (blurred + back), 0.0)

    first = pl.ds(pl.multiple_of(side * LANES, LANES), LANES)
    second = pl.ds(pl.multiple_of((1 - side) * LANES, LANES), LANES)
    count = obs.shape[0] // CHUNKS
    pieces = []
    for start in range(0, obs.shape[0], count):
        some = slice(start, start + count)
        num, back = numerator(obs[some], valid[some], counts[some]), bg[some]

        def centre(own):
            return jnp.where(left, swap(own[:, :LANES]), swap(own[:, LANES:]))

        def at_edge(own):
            return swap(jnp.where(side == 0, own[:, :LANES], own[:, LANES:]))

        straight = packed[some]
        turned = swap(straight)
        edge_num = jnp.where(from_other, jnp.where(side == 0, straight, turned), at_edge(num))
        edge_back = jnp.where(from_other, jnp.where(side == 0, turned, straight), at_edge(back))
        ratio[some, first] = divided(edge_num, edge[some] + received[some], edge_back)
        ratio[some, second] = divided(centre(num), middle[some] + other[some], centre(back))
        pieces.append(right_product(ratio[some], col_w))
    turned_ratio = jnp.concatenate(pieces, axis=0)
    store_spectrum(held, 0, to_complex(rows_forward(row_e, row_o, turned_ratio)))

    def filtered(k):
        planes = []
        a, b, c, d = load_spectrum(held, 0)
        for i in range(2):
            ha, hb, hc, hd = load_spectrum(spectrum, k + i)
            plane = from_complex(a * ha + b * hb, b * ha - a * hb, c * hc + d * hd, d * hc - c * hd)
            high, low = split(plane)
            both = dot(high, col_i[...])
            planes.append(both[:, :LANES] + (both[:, LANES:] + dot(low, col_i[:, :LANES])))
        return jnp.concatenate(planes, axis=1)

    components = weights.shape[0]
    ahead = filtered(0)
    for k in range(0, components, 2):
        planes = ahead
        if k + 2 < components:
            ahead = filtered(k + 2)
        pair = rows_inverse(inv_e, inv_o, planes, total.shape[0])
        sums = (
            side_columns(weights.at[k], side) * pair[:, :LANES]
            + side_columns(weights.at[k + 1], side) * pair[:, LANES:]
        )
        total[...] = sums if k == 0 else total[...] + sums

    result = side_columns(est, side) * total[...] / side_columns(sens, side)
    if done is None:
        updated[...] = result
    else:
        updated[:, first] = result
        updated[:, second] = done[...]


def inner_correct(*refs):
    correct_half(False, *refs)


def outer_correct(*refs):
    edge, received, middle, other, done = refs[8:13]
    correct_half(
        True, *refs[:8], edge.at[:, :LANES], received.at[:, :LANES], received.at[:, LANES:],
        middle, other, *refs[13:], done=done,
    )


def call(kernel, name, flops, args, outs, scratch, space=pltpu.VMEM):
    size = sum(a.size * a.dtype.itemsize for a in args)
    if space is pltpu.HBM:
        args = [pltpu.with_memory_space_constraint(a, pltpu.HBM) for a in args]
    return pl.pallas_call(
        kernel,
        in_specs=[pl.BlockSpec(memory_space=space)] * len(args),
        out_specs=[pl.BlockSpec(memory_space=pltpu.VMEM)] * len(outs),
        out_shape=outs,
        scratch_shapes=scratch,
        compiler_params=pltpu.CompilerParams(vmem_limit_bytes=VMEM_MIB * 2**20),
        cost_estimate=pl.CostEstimate(flops=flops // 100, bytes_accessed=size // 100, transcendentals=0),
        name=name,
    )(*args)


def local(estimate, observed, background, sensitivity, weights, kernels, valid_mask, counts):
    rows, cols = estimate.shape
    components, size = kernels.shape[0], kernels.shape[-1]
    halo = (size - 1) // 2
    half_cols = cols // 2
    row_len, col_len = rows + halo, half_cols + 2 * halo
    inner_cols = np.arange(half_cols)
    wide_cols = np.arange(-halo, half_cols + halo)
    offsets = np.arange(-halo, halo + 1)
    quarter = np.arange(row_len // 2)
    row_e, row_o = (left_table(t) for t in parity_waves(row_len, quarter))
    inv_e, inv_o = (left_table(t.T / row_len) for t in parity_waves(row_len, quarter))
    evens = -(-(halo + 1) // 16) * 16
    cos, sin = whole_waves(row_len, np.arange(halo + 1))
    cos = np.concatenate([cos, sin[:1]])
    row_c = left_table(np.pad(cos, ((0, -len(cos) % 16), (0, evens - halo - 1))))
    sin[0] = 0.0
    row_s = left_table(sin[:, 1:])
    col_h = right_table(waves(col_len, offsets).T)
    col_f = right_table(waves(col_len, inner_cols).T)
    col_w = right_table(waves(col_len, wide_cols).T)
    col_iw = right_table(waves(col_len, wide_cols) * (2.0 / col_len))
    col_i = wide_table(waves(col_len, inner_cols) * (2.0 / col_len))

    count = lax.axis_size("col")
    between = [(i, i + 1) for i in range(1, count - 1, 2)]
    between += [(j, i) for i, j in between]
    within = [(i, i ^ 1) for i in range(count)]

    macs = 3 * components * row_len * half_cols * (rows + 2 * col_len)
    plane = jax.ShapeDtypeStruct((rows, LANES), F32)
    wide = jax.ShapeDtypeStruct((rows, 2 * LANES), F32)
    spectra = jax.ShapeDtypeStruct((components, row_len, col_len), F32)
    total = pltpu.VMEM((1, row_len, col_len), F32)
    window = pltpu.VMEM((rows, col_len), F32)
    turned = jnp.transpose(kernels, (1, 0, 2))
    first = (turned, col_h, row_c, row_s)
    kept = (
        row_e, row_o, col_f, estimate, weights, col_iw, inv_e, inv_o,
        observed, background, valid_mask, counts,
    )
    columns = pltpu.VMEM(((halo + evens) * components, LANES), F32)
    spectrum, edge_o, middle_o, *kept = call(
        functools.partial(outer_blur, components), "outer_blur", 4 * macs, (*first, *kept),
        (spectra, wide, plane, *(jax.ShapeDtypeStruct(a.shape, a.dtype) for a in kept)),
        [
            *(pltpu.VMEM(a.shape, a.dtype) for a in first), columns, columns, total, window,
            pltpu.SemaphoreType.DMA((len(first) + len(kept) + 1,)),
        ],
        pltpu.HBM,
    )
    row_e, row_o, col_f, estimate, weights, col_iw, inv_e, inv_o = kept[:8]
    observed, background, valid_mask, counts = kept[8:]
    tiles = (observed, background, valid_mask, counts)
    received_o = lax.ppermute(edge_o, "col", between)
    edge_i, packed_i, middle_i = call(
        inner_blur, "inner_blur", 2 * macs,
        (estimate, *tiles, weights, spectrum, row_e, row_o, col_f, inv_e, inv_o, col_iw),
        (plane, plane, plane), [total, window],
    )
    received_i = (lax.ppermute(edge_i, "col", within), lax.ppermute(packed_i, "col", within))
    shared = (
        estimate, observed, background, sensitivity, valid_mask, counts, weights, spectrum
    )
    tables = (row_e, row_o, col_w, inv_e, inv_o, col_i)
    scratch = [window, total, pltpu.VMEM((rows, LANES), F32)]
    (half,) = call(
        inner_correct, "inner_correct", 2 * macs,
        (*shared, edge_i, *received_i, middle_i, middle_o, *tables), (plane,), scratch,
    )
    (updated,) = call(
        outer_correct, "outer_correct", 2 * macs,
        (*shared, edge_o, received_o, middle_o, middle_i, half, *tables), (wide,), scratch,
    )
    return updated


def solution(mesh):
    tile = P("group", "col")
    placed = (tile, tile, tile, tile, P(None, "group", "col"), P(), tile, tile)
    return jax.shard_map(local, mesh=mesh, in_specs=placed, out_specs=tile, check_vma=False)
```

```python
import functools

import jax
import jax.numpy as jnp
import numpy as np
from jax import lax
from jax.experimental import pallas as pl
from jax.experimental.pallas import tpu as pltpu
from jax.sharding import PartitionSpec as P

COVER = 8
LANES = 128
VMEM_MIB = 32
CHUNKS = 2
BF16 = jnp.bfloat16
F32 = jnp.float32


def halves(table):
    table = table.astype(np.float32)
    high = table.astype(jnp.bfloat16)
    return high, (table - high.astype(np.float32)).astype(jnp.bfloat16)


def waves(length, places):
    angles = 2.0 * np.pi * (np.arange(length // 2) + 0.5)[:, None] * np.asarray(places)[None, :] / length
    return np.concatenate([np.cos(angles), np.sin(angles)], axis=0)


def whole_waves(length, places):
    freqs = np.arange(length // 2)
    freqs = np.concatenate([freqs[0::2], freqs[1::2]])
    angles = 2.0 * np.pi * freqs[:, None] * np.asarray(places)[None, :] / length
    sin = np.sin(angles)
    sin[0] = np.cos(np.pi * np.asarray(places))
    return np.cos(angles), sin


def parity_waves(length, places):
    cos, sin = whole_waves(length, places)
    quarter = length // 4
    return (
        np.concatenate([cos[:quarter], sin[:quarter]]),
        np.concatenate([cos[quarter:], sin[quarter:]]),
    )


def left_table(table):
    high, low = halves(table)
    return jnp.asarray(np.concatenate([high, low, high], axis=1))


def right_table(table):
    high, low = halves(table)
    return jnp.asarray(np.concatenate([high, high, low], axis=0))


def wide_table(table):
    return jnp.asarray(np.concatenate(halves(table), axis=1))


def split(values):
    high = values.astype(BF16)
    return high, (values - high.astype(F32)).astype(BF16)


def dot(a, b):
    return jnp.dot(a, b, preferred_element_type=F32)


def left_product(table, values):
    high, low = split(values)
    return dot(table[...], jnp.concatenate([high, high, low], axis=0))


def right_product(values, table):
    high, low = split(values)
    return dot(jnp.concatenate([high, low, high], axis=1), table[...])


def rows_forward(even, odd, values):
    half = even.shape[1] // 3
    quarter = even.shape[0] // 2
    rest = values.shape[0] - half
    first, second, alone = values[:rest], values[half:], values[rest:half]
    e = left_product(even, jnp.concatenate([first + second, alone], axis=0))
    o = left_product(odd, jnp.concatenate([first - second, alone], axis=0))
    return jnp.concatenate([e[:quarter], o[:quarter], e[quarter:], o[quarter:]], axis=0)


def rows_inverse(even, odd, plane, rows):
    quarter = plane.shape[0] // 4
    parts = [plane[i * quarter:(i + 1) * quarter] for i in range(4)]
    e = left_product(even, jnp.concatenate([parts[0], parts[2]], axis=0))
    o = left_product(odd, jnp.concatenate([parts[1], parts[3]], axis=0))
    return jnp.concatenate([e + o, (e - o)[:rows - e.shape[0]]], axis=0)


def fix_first(first, values):
    row = lax.broadcasted_iota(jnp.int32, (8, 1), 0)
    return jnp.concatenate([jnp.where(row == 0, first, values[:8]), values[8:]], axis=0)


def to_complex(plane, with_first=True):
    half = plane.shape[0] // 2
    cc, cs = plane[:half, :LANES], plane[:half, LANES:]
    sc, ss = plane[half:, :LANES], plane[half:, LANES:]
    if not with_first:
        return cc - ss, cs + sc, cc + ss, cs - sc
    return (
        fix_first(cc[:8], cc - ss), fix_first(cs[:8], cs + sc),
        fix_first(sc[:8], cc + ss), fix_first(ss[:8], cs - sc),
    )


def from_complex(a, b, c, d):
    top = jnp.concatenate([fix_first(a[:8], a + c), fix_first(b[:8], b + d)], axis=1)
    low = jnp.concatenate([fix_first(c[:8], b - d), fix_first(d[:8], c - a)], axis=1)
    return jnp.concatenate([top, low], axis=0)


def store_spectrum(ref, index, parts):
    half = parts[0].shape[0]
    ref[index, :half, :LANES], ref[index, :half, LANES:] = parts[0], parts[1]
    ref[index, half:, :LANES], ref[index, half:, LANES:] = parts[2], parts[3]


def load_spectrum(ref, index):
    half = ref.shape[1] // 2
    return (
        ref[index, :half, :LANES], ref[index, :half, LANES:],
        ref[index, half:, :LANES], ref[index, half:, LANES:],
    )


def swap(values):
    return pltpu.roll(values, LANES // 2, 1)


def side_of(outer):
    core = lax.axis_index("col") % 2
    return core if outer else 1 - core


def side_columns(ref, side):
    return ref[:, pl.ds(pl.multiple_of(side * LANES, LANES), LANES)]


def numerator(obs, valid, counts):
    return valid.astype(F32) * counts.astype(F32) * (1.0 / COVER) * obs


def blur_pairs(est_half, weight_of, spectrum_of, components, row_e, row_o, col_f, total):
    def ahead(k):
        pair = jnp.concatenate([weight_of(k + i) * est_half for i in range(2)], axis=1)
        spectra = [spectrum_of(k + i) for i in range(2)]
        return rows_forward(row_e, row_o, pair), spectra

    coming = ahead(0)
    for k in range(0, components, 2):
        rows, spectra = coming
        if k + 2 < components:
            coming = ahead(k + 2)
        half = rows.shape[0] // 2
        step = half // 2
        for start in (0, step):
            sums = None
            for i in range(2):
                lanes = slice(i * LANES, (i + 1) * LANES)
                part = jnp.concatenate(
                    [rows[start:start + step, lanes], rows[half + start:half + start + step, lanes]], axis=0
                )
                fa, fb, fc, fd = to_complex(right_product(part, col_f), start == 0)
                ha, hb, hc, hd = (h[start:start + step] for h in spectra[i])
                terms = (fa * ha - fb * hb, fa * hb + fb * ha, fc * hc - fd * hd, fc * hd + fd * hc)
                sums = terms if sums is None else tuple(s + t for s, t in zip(sums, terms))
            upper, lower = slice(start, start + step), slice(half + start, half + start + step)
            places = ((upper, 0), (upper, LANES), (lower, 0), (lower, LANES))
            for (place, lane), value in zip(places, sums):
                lanes = slice(lane, lane + LANES)
                total[0, place, lanes] = value if k == 0 else total[0, place, lanes] + value


def accumulate(ref, first, sums):
    if not first:
        sums = tuple(s + t for s, t in zip(load_spectrum(ref, 0), sums))
    store_spectrum(ref, 0, sums)


def blur_end(side, obs, bg, valid, counts, inv_e, inv_o, col_i, total, edge, packed, middle, window):
    plane = rows_inverse(inv_e, inv_o, from_complex(*load_spectrum(total, 0)), window.shape[0])
    window[...] = right_product(plane, col_i)
    edge[...] = side_columns(window, side)
    middle[...] = side_columns(window, 1 - side)
    num = numerator(obs, valid, counts)
    lane = lax.broadcasted_iota(jnp.int32, (1, LANES), 1)
    num = jnp.where(side == 0, num, swap(num))
    back = jnp.where(side == 0, swap(bg), bg)
    packed[...] = jnp.where(lane < LANES // 2, num, back)


def outer_blur(components, *refs):
    inputs, refs = refs[:16], refs[16:]
    (spectrum, edge, middle), refs = refs[:3], refs[3:]
    kept, refs = refs[:12], refs[12:]
    kernels, col_h, row_c, row_s, cos_columns, sin_columns, total, window, done = refs
    columns = (cos_columns, sin_columns)
    side = side_of(True)
    near = pl.ds(pl.multiple_of(side * LANES, LANES), LANES)
    far = pl.ds(pl.multiple_of((1 - side) * LANES, LANES), LANES)
    held = (kernels, col_h, row_c, row_s, *kept)
    copies = []
    for i, (ref, own) in enumerate(zip(inputs, held)):
        if i == 8:
            copies.append((ref.at[:, :, near], own.at[:, :, near]))
        else:
            copies.append((ref, own))
    copies.append((inputs[8].at[:, :, far], held[8].at[:, :, far]))
    copies = [pltpu.make_async_copy(a, b, done.at[i]) for i, (a, b) in enumerate(copies)]
    for copy in copies[:9]:
        copy.start()
    row_e, row_o, col_f, est, weights, col_i, inv_e, inv_o, obs, bg, valid, counts = kept
    size = kernels.shape[0]
    centre = size // 2
    evens, odds = row_c.shape[1] // 3, row_s.shape[1] // 3
    half = row_s.shape[0]
    copies[0].wait()
    copies[1].wait()
    above, below = kernels[centre + 1:], [kernels[i:i + 1] for i in range(centre - 1, -1, -1)]
    below = jnp.concatenate(below, axis=0)
    turned = (above - below, jnp.concatenate([kernels[centre:centre + 1], above + below], axis=0))
    start = 0
    for folded in turned:
        flat = folded.reshape(-1, size)
        plane = right_product(flat, col_h)
        for part, ref in enumerate(columns):
            ref[start:start + len(flat)] = plane[:, part * LANES:(part + 1) * LANES]
        start += len(flat)
    empty = (odds + evens - size) * components
    for ref in columns:
        ref[start:] = jnp.zeros((empty, LANES), F32)
    for copy in copies[2:9]:
        copy.wait()
    for copy in copies[9:]:
        copy.start()

    def spectrum_of(k):
        def taken(start, count):
            places = pl.ds(k + start * components, count, stride=components)
            return jnp.concatenate([ref[places, :] for ref in columns], axis=1)

        cos = left_product(row_c, taken(odds, evens))
        sin = left_product(row_s, taken(0, odds))
        sin = fix_first(cos[half:half + 1], sin)
        parts = to_complex(jnp.concatenate([cos[:half], sin], axis=0))
        store_spectrum(spectrum, k, parts)
        return parts

    blur_pairs(
        side_columns(est, side), lambda k: side_columns(weights.at[k], side), spectrum_of,
        components, row_e, row_o, col_f, total,
    )
    for copy in copies[9:]:
        copy.wait()
    tiles = (side_columns(ref, side) for ref in (obs, bg, valid, counts))
    blur_end(
        side, *tiles, inv_e, inv_o, col_i, total,
        edge.at[:, :LANES], edge.at[:, LANES:], middle, window,
    )


def inner_blur(
    est, obs, bg, valid, counts, weights, spectrum, row_e, row_o, col_f, inv_e, inv_o, col_i,
    edge, packed, middle, total, window,
):
    side = side_of(False)
    blur_pairs(
        side_columns(est, side), lambda k: side_columns(weights.at[k], side),
        lambda k: load_spectrum(spectrum, k), weights.shape[0], row_e, row_o, col_f, total,
    )
    tiles = (side_columns(ref, side) for ref in (obs, bg, valid, counts))
    blur_end(side, *tiles, inv_e, inv_o, col_i, total, edge, packed, middle, window)


def correct_half(
    outer, est, obs, bg, sens, valid, counts, weights, spectrum, edge, received, packed, middle, other,
    row_e, row_o, col_w, inv_e, inv_o, col_i, updated, ratio, held, total, done=None,
):
    side = side_of(outer)
    lane = lax.broadcasted_iota(jnp.int32, (1, LANES), 1)
    left = lane < LANES // 2
    from_other = (lane >= LANES // 2) == (side == 1)

    def divided(num, blurred, back):
        return jnp.where(num > 0.0, num / (blurred + back), 0.0)

    first = pl.ds(pl.multiple_of(side * LANES, LANES), LANES)
    second = pl.ds(pl.multiple_of((1 - side) * LANES, LANES), LANES)
    count = obs.shape[0] // CHUNKS
    pieces = []
    for start in range(0, obs.shape[0], count):
        some = slice(start, start + count)
        num, back = numerator(obs[some], valid[some], counts[some]), bg[some]

        def centre(own):
            return jnp.where(left, swap(own[:, :LANES]), swap(own[:, LANES:]))

        def at_edge(own):
            return swap(jnp.where(side == 0, own[:, :LANES], own[:, LANES:]))

        straight = packed[some]
        turned = swap(straight)
        edge_num = jnp.where(from_other, jnp.where(side == 0, straight, turned), at_edge(num))
        edge_back = jnp.where(from_other, jnp.where(side == 0, turned, straight), at_edge(back))
        ratio[some, first] = divided(edge_num, edge[some] + received[some], edge_back)
        ratio[some, second] = divided(centre(num), middle[some] + other[some], centre(back))
        pieces.append(right_product(ratio[some], col_w))
    turned_ratio = jnp.concatenate(pieces, axis=0)
    store_spectrum(held, 0, to_complex(rows_forward(row_e, row_o, turned_ratio)))

    def filtered(k):
        planes = []
        a, b, c, d = load_spectrum(held, 0)
        for i in range(2):
            ha, hb, hc, hd = load_spectrum(spectrum, k + i)
            plane = from_complex(a * ha + b * hb, b * ha - a * hb, c * hc + d * hd, d * hc - c * hd)
            high, low = split(plane)
            both = dot(high, col_i[...])
            planes.append(both[:, :LANES] + (both[:, LANES:] + dot(low, col_i[:, :LANES])))
        return jnp.concatenate(planes, axis=1)

    components = weights.shape[0]
    ahead = filtered(0)
    for k in range(0, components, 2):
        planes = ahead
        if k + 2 < components:
            ahead = filtered(k + 2)
        pair = rows_inverse(inv_e, inv_o, planes, total.shape[0])
        sums = (
            side_columns(weights.at[k], side) * pair[:, :LANES]
            + side_columns(weights.at[k + 1], side) * pair[:, LANES:]
        )
        total[...] = sums if k == 0 else total[...] + sums

    result = side_columns(est, side) * total[...] / side_columns(sens, side)
    if done is None:
        updated[...] = result
    else:
        updated[:, first] = result
        updated[:, second] = done[...]


def inner_correct(*refs):
    correct_half(False, *refs)


def outer_correct(*refs):
    edge, received, middle, other, done = refs[8:13]
    correct_half(
        True, *refs[:8], edge.at[:, :LANES], received.at[:, :LANES], received.at[:, LANES:],
        middle, other, *refs[13:], done=done,
    )


def call(kernel, name, flops, args, outs, scratch, space=pltpu.VMEM):
    size = sum(a.size * a.dtype.itemsize for a in args)
    if space is pltpu.HBM:
        args = [pltpu.with_memory_space_constraint(a, pltpu.HBM) for a in args]
    return pl.pallas_call(
        kernel,
        in_specs=[pl.BlockSpec(memory_space=space)] * len(args),
        out_specs=[pl.BlockSpec(memory_space=pltpu.VMEM)] * len(outs),
        out_shape=outs,
        scratch_shapes=scratch,
        compiler_params=pltpu.CompilerParams(vmem_limit_bytes=VMEM_MIB * 2**20),
        cost_estimate=pl.CostEstimate(flops=flops // 100, bytes_accessed=size // 100, transcendentals=0),
        name=name,
    )(*args)


def local(estimate, observed, background, sensitivity, weights, kernels, valid_mask, counts):
    rows, cols = estimate.shape
    components, size = kernels.shape[0], kernels.shape[-1]
    halo = (size - 1) // 2
    half_cols = cols // 2
    row_len, col_len = rows + halo, half_cols + 2 * halo
    inner_cols = np.arange(half_cols)
    wide_cols = np.arange(-halo, half_cols + halo)
    offsets = np.arange(-halo, halo + 1)
    quarter = np.arange(row_len // 2)
    row_e, row_o = (left_table(t) for t in parity_waves(row_len, quarter))
    inv_e, inv_o = (left_table(t.T / row_len) for t in parity_waves(row_len, quarter))
    evens = -(-(halo + 1) // 16) * 16
    cos, sin = whole_waves(row_len, np.arange(halo + 1))
    cos = np.concatenate([cos, sin[:1]])
    row_c = left_table(np.pad(cos, ((0, -len(cos) % 16), (0, evens - halo - 1))))
    sin[0] = 0.0
    row_s = left_table(sin[:, 1:])
    col_h = right_table(waves(col_len, offsets).T)
    col_f = right_table(waves(col_len, inner_cols).T)
    col_w = right_table(waves(col_len, wide_cols).T)
    col_iw = right_table(waves(col_len, wide_cols) * (2.0 / col_len))
    col_i = wide_table(waves(col_len, inner_cols) * (2.0 / col_len))

    count = lax.axis_size("col")
    between = [(i, i + 1) for i in range(1, count - 1, 2)]
    between += [(j, i) for i, j in between]
    within = [(i, i ^ 1) for i in range(count)]

    macs = 3 * components * row_len * half_cols * (rows + 2 * col_len)
    plane = jax.ShapeDtypeStruct((rows, LANES), F32)
    wide = jax.ShapeDtypeStruct((rows, 2 * LANES), F32)
    spectra = jax.ShapeDtypeStruct((components, row_len, col_len), F32)
    total = pltpu.VMEM((1, row_len, col_len), F32)
    window = pltpu.VMEM((rows, col_len), F32)
    turned = jnp.transpose(kernels, (1, 0, 2))
    first = (turned, col_h, row_c, row_s)
    kept = (
        row_e, row_o, col_f, estimate, weights, col_iw, inv_e, inv_o,
        observed, background, valid_mask, counts,
    )
    columns = pltpu.VMEM(((halo + evens) * components, LANES), F32)
    spectrum, edge_o, middle_o, *kept = call(
        functools.partial(outer_blur, components), "outer_blur", 4 * macs, (*first, *kept),
        (spectra, wide, plane, *(jax.ShapeDtypeStruct(a.shape, a.dtype) for a in kept)),
        [
            *(pltpu.VMEM(a.shape, a.dtype) for a in first), columns, columns, total, window,
            pltpu.SemaphoreType.DMA((len(first) + len(kept) + 1,)),
        ],
        pltpu.HBM,
    )
    row_e, row_o, col_f, estimate, weights, col_iw, inv_e, inv_o = kept[:8]
    observed, background, valid_mask, counts = kept[8:]
    tiles = (observed, background, valid_mask, counts)
    received_o = lax.ppermute(edge_o, "col", between)
    edge_i, packed_i, middle_i = call(
        inner_blur, "inner_blur", 2 * macs,
        (estimate, *tiles, weights, spectrum, row_e, row_o, col_f, inv_e, inv_o, col_iw),
        (plane, plane, plane), [total, window],
    )
    received_i = (lax.ppermute(edge_i, "col", within), lax.ppermute(packed_i, "col", within))
    shared = (
        estimate, observed, background, sensitivity, valid_mask, counts, weights, spectrum
    )
    tables = (row_e, row_o, col_w, inv_e, inv_o, col_i)
    scratch = [window, total, pltpu.VMEM((rows, LANES), F32)]
    (half,) = call(
        inner_correct, "inner_correct", 2 * macs,
        (*shared, edge_i, *received_i, middle_i, middle_o, *tables), (plane,), scratch,
    )
    (updated,) = call(
        outer_correct, "outer_correct", 2 * macs,
        (*shared, edge_o, received_o, middle_o, middle_i, half, *tables), (wide,), scratch,
    )
    return updated


def solution(mesh):
    tile = P("group", "col")
    placed = (tile, tile, tile, tile, P(None, "group", "col"), P(), tile, tile)
    return jax.shard_map(local, mesh=mesh, in_specs=placed, out_specs=tile, check_vma=False)
```

```python
import functools

import jax
import jax.numpy as jnp
import numpy as np
from jax import lax
from jax.experimental import pallas as pl
from jax.experimental.pallas import tpu as pltpu
from jax.sharding import PartitionSpec as P

COVER = 8
LANES = 128
VMEM_MIB = 32
CHUNKS = 2
BF16 = jnp.bfloat16
F32 = jnp.float32


def halves(table):
    table = table.astype(np.float32)
    high = table.astype(jnp.bfloat16)
    return high, (table - high.astype(np.float32)).astype(jnp.bfloat16)


def waves(length, places):
    angles = 2.0 * np.pi * (np.arange(length // 2) + 0.5)[:, None] * np.asarray(places)[None, :] / length
    return np.concatenate([np.cos(angles), np.sin(angles)], axis=0)


def whole_waves(length, places):
    freqs = np.arange(length // 2)
    freqs = np.concatenate([freqs[0::2], freqs[1::2]])
    angles = 2.0 * np.pi * freqs[:, None] * np.asarray(places)[None, :] / length
    sin = np.sin(angles)
    sin[0] = np.cos(np.pi * np.asarray(places))
    return np.cos(angles), sin


def parity_waves(length, places):
    cos, sin = whole_waves(length, places)
    quarter = length // 4
    return (
        np.concatenate([cos[:quarter], sin[:quarter]]),
        np.concatenate([cos[quarter:], sin[quarter:]]),
    )


def left_table(table):
    high, low = halves(table)
    return jnp.asarray(np.concatenate([high, low, high], axis=1))


def right_table(table):
    high, low = halves(table)
    return jnp.asarray(np.concatenate([high, high, low], axis=0))


def wide_table(table):
    return jnp.asarray(np.concatenate(halves(table), axis=1))


def split(values):
    high = values.astype(BF16)
    return high, (values - high.astype(F32)).astype(BF16)


def dot(a, b):
    return jnp.dot(a, b, preferred_element_type=F32)


def left_product(table, values):
    high, low = split(values)
    return dot(table[...], jnp.concatenate([high, high, low], axis=0))


def right_product(values, table):
    high, low = split(values)
    return dot(jnp.concatenate([high, low, high], axis=1), table[...])


def rows_forward(even, odd, values):
    half = even.shape[1] // 3
    quarter = even.shape[0] // 2
    rest = values.shape[0] - half
    first, second, alone = values[:rest], values[half:], values[rest:half]
    e = left_product(even, jnp.concatenate([first + second, alone], axis=0))
    o = left_product(odd, jnp.concatenate([first - second, alone], axis=0))
    return jnp.concatenate([e[:quarter], o[:quarter], e[quarter:], o[quarter:]], axis=0)


def rows_inverse(even, odd, plane, rows):
    quarter = plane.shape[0] // 4
    parts = [plane[i * quarter:(i + 1) * quarter] for i in range(4)]
    e = left_product(even, jnp.concatenate([parts[0], parts[2]], axis=0))
    o = left_product(odd, jnp.concatenate([parts[1], parts[3]], axis=0))
    return jnp.concatenate([e + o, (e - o)[:rows - e.shape[0]]], axis=0)


def fix_first(first, values):
    row = lax.broadcasted_iota(jnp.int32, (8, 1), 0)
    return jnp.concatenate([jnp.where(row == 0, first, values[:8]), values[8:]], axis=0)


def to_complex(plane, with_first=True):
    half = plane.shape[0] // 2
    cc, cs = plane[:half, :LANES], plane[:half, LANES:]
    sc, ss = plane[half:, :LANES], plane[half:, LANES:]
    if not with_first:
        return cc - ss, cs + sc, cc + ss, cs - sc
    return (
        fix_first(cc[:8], cc - ss), fix_first(cs[:8], cs + sc),
        fix_first(sc[:8], cc + ss), fix_first(ss[:8], cs - sc),
    )


def from_complex(a, b, c, d, with_first=True):
    if not with_first:
        top = jnp.concatenate([a + c, b + d], axis=1)
        return jnp.concatenate([top, jnp.concatenate([b - d, c - a], axis=1)], axis=0)
    top = jnp.concatenate([fix_first(a[:8], a + c), fix_first(b[:8], b + d)], axis=1)
    low = jnp.concatenate([fix_first(c[:8], b - d), fix_first(d[:8], c - a)], axis=1)
    return jnp.concatenate([top, low], axis=0)


def store_spectrum(ref, index, parts):
    half = parts[0].shape[0]
    ref[index, :half, :LANES], ref[index, :half, LANES:] = parts[0], parts[1]
    ref[index, half:, :LANES], ref[index, half:, LANES:] = parts[2], parts[3]


def load_spectrum(ref, index):
    half = ref.shape[1] // 2
    return (
        ref[index, :half, :LANES], ref[index, :half, LANES:],
        ref[index, half:, :LANES], ref[index, half:, LANES:],
    )


def swap(values):
    return pltpu.roll(values, LANES // 2, 1)


def side_of(outer):
    core = lax.axis_index("col") % 2
    return core if outer else 1 - core


def side_columns(ref, side):
    return ref[:, pl.ds(pl.multiple_of(side * LANES, LANES), LANES)]


def numerator(obs, valid, counts):
    return valid.astype(F32) * counts.astype(F32) * (1.0 / COVER) * obs


def blur_pairs(est_half, weight_of, spectrum_of, components, row_e, row_o, col_f, total):
    def ahead(k):
        pair = jnp.concatenate([weight_of(k + i) * est_half for i in range(2)], axis=1)
        spectra = [spectrum_of(k + i) for i in range(2)]
        return rows_forward(row_e, row_o, pair), spectra

    coming = ahead(0)
    for k in range(0, components, 2):
        rows, spectra = coming
        if k + 2 < components:
            coming = ahead(k + 2)
        half = rows.shape[0] // 2
        step = half // 2
        for start in (0, step):
            sums = None
            for i in range(2):
                lanes = slice(i * LANES, (i + 1) * LANES)
                part = jnp.concatenate(
                    [rows[start:start + step, lanes], rows[half + start:half + start + step, lanes]], axis=0
                )
                fa, fb, fc, fd = to_complex(right_product(part, col_f), start == 0)
                ha, hb, hc, hd = (h[start:start + step] for h in spectra[i])
                terms = (fa * ha - fb * hb, fa * hb + fb * ha, fc * hc - fd * hd, fc * hd + fd * hc)
                sums = terms if sums is None else tuple(s + t for s, t in zip(sums, terms))
            upper, lower = slice(start, start + step), slice(half + start, half + start + step)
            places = ((upper, 0), (upper, LANES), (lower, 0), (lower, LANES))
            for (place, lane), value in zip(places, sums):
                lanes = slice(lane, lane + LANES)
                total[0, place, lanes] = value if k == 0 else total[0, place, lanes] + value


def accumulate(ref, first, sums):
    if not first:
        sums = tuple(s + t for s, t in zip(load_spectrum(ref, 0), sums))
    store_spectrum(ref, 0, sums)


def blur_end(side, obs, bg, valid, counts, inv_e, inv_o, col_i, total, edge, packed, middle, window):
    plane = rows_inverse(inv_e, inv_o, from_complex(*load_spectrum(total, 0)), window.shape[0])
    window[...] = right_product(plane, col_i)
    edge[...] = side_columns(window, side)
    middle[...] = side_columns(window, 1 - side)
    num = numerator(obs, valid, counts)
    lane = lax.broadcasted_iota(jnp.int32, (1, LANES), 1)
    num = jnp.where(side == 0, num, swap(num))
    back = jnp.where(side == 0, swap(bg), bg)
    packed[...] = jnp.where(lane < LANES // 2, num, back)


def outer_blur(components, *refs):
    inputs, refs = refs[:16], refs[16:]
    (spectrum, edge, middle), refs = refs[:3], refs[3:]
    kept, refs = refs[:12], refs[12:]
    kernels, col_h, row_c, row_s, cos_columns, sin_columns, total, window, done = refs
    columns = (cos_columns, sin_columns)
    side = side_of(True)
    near = pl.ds(pl.multiple_of(side * LANES, LANES), LANES)
    far = pl.ds(pl.multiple_of((1 - side) * LANES, LANES), LANES)
    held = (kernels, col_h, row_c, row_s, *kept)
    copies = []
    for i, (ref, own) in enumerate(zip(inputs, held)):
        if i == 8:
            copies.append((ref.at[:, :, near], own.at[:, :, near]))
        else:
            copies.append((ref, own))
    copies.append((inputs[8].at[:, :, far], held[8].at[:, :, far]))
    copies = [pltpu.make_async_copy(a, b, done.at[i]) for i, (a, b) in enumerate(copies)]
    for copy in copies[:9]:
        copy.start()
    row_e, row_o, col_f, est, weights, col_i, inv_e, inv_o, obs, bg, valid, counts = kept
    size = kernels.shape[0]
    centre = size // 2
    evens, odds = row_c.shape[1] // 3, row_s.shape[1] // 3
    half = row_s.shape[0]
    copies[0].wait()
    copies[1].wait()
    above, below = kernels[centre + 1:], [kernels[i:i + 1] for i in range(centre - 1, -1, -1)]
    below = jnp.concatenate(below, axis=0)
    turned = (above - below, jnp.concatenate([kernels[centre:centre + 1], above + below], axis=0))
    start = 0
    for folded in turned:
        flat = folded.reshape(-1, size)
        plane = right_product(flat, col_h)
        for part, ref in enumerate(columns):
            ref[start:start + len(flat)] = plane[:, part * LANES:(part + 1) * LANES]
        start += len(flat)
    empty = (odds + evens - size) * components
    for ref in columns:
        ref[start:] = jnp.zeros((empty, LANES), F32)
    for copy in copies[2:9]:
        copy.wait()
    for copy in copies[9:]:
        copy.start()

    def spectrum_of(k):
        def taken(start, count):
            places = pl.ds(k + start * components, count, stride=components)
            return jnp.concatenate([ref[places, :] for ref in columns], axis=1)

        cos = left_product(row_c, taken(odds, evens))
        sin = left_product(row_s, taken(0, odds))
        sin = fix_first(cos[half:half + 1], sin)
        parts = to_complex(jnp.concatenate([cos[:half], sin], axis=0))
        store_spectrum(spectrum, k, parts)
        return parts

    blur_pairs(
        side_columns(est, side), lambda k: side_columns(weights.at[k], side), spectrum_of,
        components, row_e, row_o, col_f, total,
    )
    for copy in copies[9:]:
        copy.wait()
    tiles = (side_columns(ref, side) for ref in (obs, bg, valid, counts))
    blur_end(
        side, *tiles, inv_e, inv_o, col_i, total,
        edge.at[:, :LANES], edge.at[:, LANES:], middle, window,
    )


def inner_blur(
    est, obs, bg, valid, counts, weights, spectrum, row_e, row_o, col_f, inv_e, inv_o, col_i,
    edge, packed, middle, total, window,
):
    side = side_of(False)
    blur_pairs(
        side_columns(est, side), lambda k: side_columns(weights.at[k], side),
        lambda k: load_spectrum(spectrum, k), weights.shape[0], row_e, row_o, col_f, total,
    )
    tiles = (side_columns(ref, side) for ref in (obs, bg, valid, counts))
    blur_end(side, *tiles, inv_e, inv_o, col_i, total, edge, packed, middle, window)


def correct_half(
    outer, est, obs, bg, sens, valid, counts, weights, spectrum, edge, received, packed, middle, other,
    row_e, row_o, col_w, inv_e, inv_o, col_i, updated, ratio, held, total, done=None,
):
    side = side_of(outer)
    lane = lax.broadcasted_iota(jnp.int32, (1, LANES), 1)
    left = lane < LANES // 2
    from_other = (lane >= LANES // 2) == (side == 1)

    def divided(num, blurred, back):
        return jnp.where(num > 0.0, num / (blurred + back), 0.0)

    first = pl.ds(pl.multiple_of(side * LANES, LANES), LANES)
    second = pl.ds(pl.multiple_of((1 - side) * LANES, LANES), LANES)
    count = obs.shape[0] // CHUNKS
    pieces = []
    for start in range(0, obs.shape[0], count):
        some = slice(start, start + count)
        num, back = numerator(obs[some], valid[some], counts[some]), bg[some]

        def centre(own):
            return jnp.where(left, swap(own[:, :LANES]), swap(own[:, LANES:]))

        def at_edge(own):
            return swap(jnp.where(side == 0, own[:, :LANES], own[:, LANES:]))

        straight = packed[some]
        turned = swap(straight)
        edge_num = jnp.where(from_other, jnp.where(side == 0, straight, turned), at_edge(num))
        edge_back = jnp.where(from_other, jnp.where(side == 0, turned, straight), at_edge(back))
        ratio[some, first] = divided(edge_num, edge[some] + received[some], edge_back)
        ratio[some, second] = divided(centre(num), middle[some] + other[some], centre(back))
        pieces.append(right_product(ratio[some], col_w))
    turned_ratio = jnp.concatenate(pieces, axis=0)
    store_spectrum(held, 0, to_complex(rows_forward(row_e, row_o, turned_ratio)))

    def filtered(k):
        spectra = load_spectrum(held, 0)
        half = spectra[0].shape[0]
        step = half // 2
        planes = []
        for i in range(2):
            kernel = load_spectrum(spectrum, k + i)
            pieces = []
            for start in (0, step):
                rows = slice(start, start + step)
                a, b, c, d = (x[rows] for x in spectra)
                ha, hb, hc, hd = (x[rows] for x in kernel)
                parts = (a * ha + b * hb, b * ha - a * hb, c * hc + d * hd, d * hc - c * hd)
                high, low = split(from_complex(*parts, start == 0))
                both = dot(high, col_i[...])
                pieces.append(both[:, :LANES] + (both[:, LANES:] + dot(low, col_i[:, :LANES])))
            upper, lower = [p[:step] for p in pieces], [p[step:] for p in pieces]
            planes.append(jnp.concatenate(upper + lower, axis=0))
        return jnp.concatenate(planes, axis=1)

    components = weights.shape[0]
    ahead = filtered(0)
    for k in range(0, components, 2):
        planes = ahead
        if k + 2 < components:
            ahead = filtered(k + 2)
        pair = rows_inverse(inv_e, inv_o, planes, total.shape[0])
        sums = (
            side_columns(weights.at[k], side) * pair[:, :LANES]
            + side_columns(weights.at[k + 1], side) * pair[:, LANES:]
        )
        total[...] = sums if k == 0 else total[...] + sums

    result = side_columns(est, side) * total[...] / side_columns(sens, side)
    if done is None:
        updated[...] = result
    else:
        updated[:, first] = result
        updated[:, second] = done[...]


def inner_correct(*refs):
    correct_half(False, *refs)


def outer_correct(*refs):
    edge, received, middle, other, done = refs[8:13]
    correct_half(
        True, *refs[:8], edge.at[:, :LANES], received.at[:, :LANES], received.at[:, LANES:],
        middle, other, *refs[13:], done=done,
    )


def call(kernel, name, flops, args, outs, scratch, space=pltpu.VMEM):
    size = sum(a.size * a.dtype.itemsize for a in args)
    if space is pltpu.HBM:
        args = [pltpu.with_memory_space_constraint(a, pltpu.HBM) for a in args]
    return pl.pallas_call(
        kernel,
        in_specs=[pl.BlockSpec(memory_space=space)] * len(args),
        out_specs=[pl.BlockSpec(memory_space=pltpu.VMEM)] * len(outs),
        out_shape=outs,
        scratch_shapes=scratch,
        compiler_params=pltpu.CompilerParams(vmem_limit_bytes=VMEM_MIB * 2**20),
        cost_estimate=pl.CostEstimate(flops=flops // 100, bytes_accessed=size // 100, transcendentals=0),
        name=name,
    )(*args)


def local(estimate, observed, background, sensitivity, weights, kernels, valid_mask, counts):
    rows, cols = estimate.shape
    components, size = kernels.shape[0], kernels.shape[-1]
    halo = (size - 1) // 2
    half_cols = cols // 2
    row_len, col_len = rows + halo, half_cols + 2 * halo
    inner_cols = np.arange(half_cols)
    wide_cols = np.arange(-halo, half_cols + halo)
    offsets = np.arange(-halo, halo + 1)
    quarter = np.arange(row_len // 2)
    row_e, row_o = (left_table(t) for t in parity_waves(row_len, quarter))
    inv_e, inv_o = (left_table(t.T / row_len) for t in parity_waves(row_len, quarter))
    evens = -(-(halo + 1) // 16) * 16
    cos, sin = whole_waves(row_len, np.arange(halo + 1))
    cos = np.concatenate([cos, sin[:1]])
    row_c = left_table(np.pad(cos, ((0, -len(cos) % 16), (0, evens - halo - 1))))
    sin[0] = 0.0
    row_s = left_table(sin[:, 1:])
    col_h = right_table(waves(col_len, offsets).T)
    col_f = right_table(waves(col_len, inner_cols).T)
    col_w = right_table(waves(col_len, wide_cols).T)
    col_iw = right_table(waves(col_len, wide_cols) * (2.0 / col_len))
    col_i = wide_table(waves(col_len, inner_cols) * (2.0 / col_len))

    count = lax.axis_size("col")
    between = [(i, i + 1) for i in range(1, count - 1, 2)]
    between += [(j, i) for i, j in between]
    within = [(i, i ^ 1) for i in range(count)]

    macs = 3 * components * row_len * half_cols * (rows + 2 * col_len)
    plane = jax.ShapeDtypeStruct((rows, LANES), F32)
    wide = jax.ShapeDtypeStruct((rows, 2 * LANES), F32)
    spectra = jax.ShapeDtypeStruct((components, row_len, col_len), F32)
    total = pltpu.VMEM((1, row_len, col_len), F32)
    window = pltpu.VMEM((rows, col_len), F32)
    turned = jnp.transpose(kernels, (1, 0, 2))
    first = (turned, col_h, row_c, row_s)
    kept = (
        row_e, row_o, col_f, estimate, weights, col_iw, inv_e, inv_o,
        observed, background, valid_mask, counts,
    )
    columns = pltpu.VMEM(((halo + evens) * components, LANES), F32)
    spectrum, edge_o, middle_o, *kept = call(
        functools.partial(outer_blur, components), "outer_blur", 4 * macs, (*first, *kept),
        (spectra, wide, plane, *(jax.ShapeDtypeStruct(a.shape, a.dtype) for a in kept)),
        [
            *(pltpu.VMEM(a.shape, a.dtype) for a in first), columns, columns, total, window,
            pltpu.SemaphoreType.DMA((len(first) + len(kept) + 1,)),
        ],
        pltpu.HBM,
    )
    row_e, row_o, col_f, estimate, weights, col_iw, inv_e, inv_o = kept[:8]
    observed, background, valid_mask, counts = kept[8:]
    tiles = (observed, background, valid_mask, counts)
    received_o = lax.ppermute(edge_o, "col", between)
    edge_i, packed_i, middle_i = call(
        inner_blur, "inner_blur", 2 * macs,
        (estimate, *tiles, weights, spectrum, row_e, row_o, col_f, inv_e, inv_o, col_iw),
        (plane, plane, plane), [total, window],
    )
    received_i = (lax.ppermute(edge_i, "col", within), lax.ppermute(packed_i, "col", within))
    shared = (
        estimate, observed, background, sensitivity, valid_mask, counts, weights, spectrum
    )
    tables = (row_e, row_o, col_w, inv_e, inv_o, col_i)
    scratch = [window, total, pltpu.VMEM((rows, LANES), F32)]
    (half,) = call(
        inner_correct, "inner_correct", 2 * macs,
        (*shared, edge_i, *received_i, middle_i, middle_o, *tables), (plane,), scratch,
    )
    (updated,) = call(
        outer_correct, "outer_correct", 2 * macs,
        (*shared, edge_o, received_o, middle_o, middle_i, half, *tables), (wide,), scratch,
    )
    return updated


def solution(mesh):
    tile = P("group", "col")
    placed = (tile, tile, tile, tile, P(None, "group", "col"), P(), tile, tile)
    return jax.shard_map(local, mesh=mesh, in_specs=placed, out_specs=tile, check_vma=False)
```
